32 devices in a mesh: seq: 8 (over y, x, core), head: 4 (over z).
Axes of the slice: x: 2, y: 2, z: 4, core: 2. Of those that a mesh axis runs over, the one named last changes fastest.
Arguments:
- main_query: bfloat16 [1024, 73728], P('seq', 'head'), may hold values from -18 to 18
- latent: bfloat16 [2048, 576], P('seq'), may hold values from -6 to 6
- main_outside: float32 [1024, 128], P('seq', 'head'), may hold values from 5 to 11
- index_query: bfloat16 [1024, 8192], P('seq', 'head'), may hold values from -6 to 6
- index_weights: float32 [1024, 64], P('seq', 'head'), may hold values from -2.4 to 2.4
- index_keys: bfloat16 [2048, 128], P('seq'), may hold values from -6 to 6
- index_outside: float32 [1024], P('seq'), may hold values from 6 to 10
- query_pos: int32 [1024], P('seq'), may hold values from 1 to 4095, as said below
- key_pos: int32 [2048], P('seq'), may hold values from 0 to 4095, as said below
Outputs:
- grad_index_query: bfloat16 [1024, 8192], P('seq', 'head')
- grad_index_weights: float32 [1024, 64], P('seq', 'head')
- grad_index_keys: float32 [2048, 128], P('seq')
The draws below stay inside these ranges and needn't reach their ends.
Inputs may be any that keep to these rules, and one draw needn't show every extreme that they name: `key_pos`: key j of block b stands at 2 * 256 * b + 2 * j or one more; key 0 of a block at 2 * 256 * b exactly. `query_pos`: queries of block b stand at 2 * 256 * b + 1 to 2 * 256 * b + 2 * 256 - 1.
All inputs are finite; a program needn't handle non-finite values.
Results may differ from the reference program's by a relative error of at most 0.00205.
Values may be sent and summed in bfloat16 or wider, within the bound.
No kernel may reach another device: no remote copies, remote signals or barrier semaphores. Data moves between devices by JAX's collectives and lax.ppermute only.
A program may use at most 128 MiB of HBM per device.

```python
import jax
import jax.numpy as jnp
from jax import lax

HEADS = 128
LAT = 512
ROPE = 64
IHEADS = 64
IDIM = 128
Q_DEV = 128
KB = 256
STEPS = 4
QUERIES = 1024
KEYS = 2048
N_SEQ = 8


def draw_main_query(key, part):
    width = LAT + ROPE
    own_key = jax.random.fold_in(key, 31)
    base = jnp.clip(jax.random.normal(own_key, (QUERIES, HEADS, width), jnp.float32), -6.0, 6.0)
    return base.reshape(QUERIES, HEADS * width).astype(jnp.bfloat16)


def draw_latent(key, part):
    width = LAT + ROPE
    own_key = jax.random.fold_in(key, 37)
    base = jnp.clip(jax.random.normal(own_key, (KEYS, width), jnp.float32), -6.0, 6.0)
    return base.astype(jnp.bfloat16)


def draw_index_query(key, part):
    own_key = jax.random.fold_in(key, 41)
    base = jnp.clip(jax.random.normal(own_key, (QUERIES, IHEADS, IDIM), jnp.float32), -6.0, 6.0)
    return base.reshape(QUERIES, IHEADS * IDIM).astype(jnp.bfloat16)


def draw_index_weights(key, part):
    own_key = jax.random.fold_in(key, 43)
    base = jnp.clip(0.4 * jax.random.normal(own_key, (QUERIES, IHEADS), jnp.float32), -2.4, 2.4)
    return base.astype(jnp.float32)


def draw_index_keys(key, part):
    own_key = jax.random.fold_in(key, 47)
    base = jnp.clip(jax.random.normal(own_key, (KEYS, IDIM), jnp.float32), -6.0, 6.0)
    return base.astype(jnp.bfloat16)


def draw_key_pos(key, part):
    places = jnp.arange(KEYS, dtype=jnp.int32)
    inner = places % KB
    coins = jax.random.randint(jax.random.fold_in(key, 11), (KEYS,), 0, 2, dtype=jnp.int32)
    coins = jnp.where(inner == 0, 0, jnp.where(inner == KB - 1, 1, coins))
    return (places // KB * 2 * KB + 2 * inner + coins).astype(jnp.int32)


def draw_query_pos(key, part):
    places = jnp.arange(QUERIES, dtype=jnp.int32)
    inner = places % Q_DEV
    offsets = jax.random.randint(jax.random.fold_in(key, 13), (QUERIES,), 1, 2 * KB, dtype=jnp.int32)
    offsets = jnp.where(inner == 0, 1, jnp.where(inner == Q_DEV - 1, 2 * KB - 1, offsets))
    return (places // Q_DEV * 2 * KB + offsets).astype(jnp.int32)


def steps_of(rng, shape, shards, least, largest):
    level = 1.0
    for axis_at, parts in shards:
        draws = jax.random.uniform(jax.random.fold_in(jax.random.fold_in(rng, 6), axis_at), (parts,), jnp.float32, least / len(shards), largest / len(shards))
        level = level * jnp.repeat(jnp.exp(draws), shape[axis_at] // parts).reshape((-1,) + (1,) * (len(shape) - 1 - axis_at))
    return level


def setup_inputs(seed: int = 0) -> dict:
    key_of = jax.random.split(jax.random.key(seed), 10)
    return {
        "main_query": draw_main_query(jax.random.fold_in(key_of[9], 71), 0),
        "latent": draw_latent(jax.random.fold_in(key_of[9], 71), 0),
        "main_outside": jnp.clip(5.0 + 6.0 * jax.random.uniform(key_of[2], (QUERIES, HEADS), jnp.float32) ** steps_of(key_of[2], (QUERIES, HEADS), ((0, 8), (1, 4)), -0.2, 0.2), 5.0, 11.0),
        "index_query": draw_index_query(jax.random.fold_in(key_of[9], 71), 0),
        "index_weights": draw_index_weights(jax.random.fold_in(key_of[9], 71), 0),
        "index_keys": draw_index_keys(jax.random.fold_in(key_of[9], 71), 0),
        "index_outside": jnp.clip(6.0 + 4.0 * jax.random.uniform(key_of[6], (QUERIES,), jnp.float32) ** steps_of(key_of[6], (QUERIES,), ((0, 8),), -0.2, 0.2), 6.0, 10.0),
        "query_pos": draw_query_pos(jax.random.fold_in(key_of[9], 71), 0),
        "key_pos": draw_key_pos(jax.random.fold_in(key_of[9], 71), 0),
    }


NEGATIVE = -1e+30
SCORE_SCALE = 192.0 ** (-0.5)

def head_mass(scores, visible, outside):
    masked = jnp.where(visible[None], scores, NEGATIVE)
    highest = jnp.maximum(lax.optimization_barrier(jnp.max(masked, axis=2)), outside.T)
    expo = jnp.exp(masked - highest[:, :, None])
    total = lax.optimization_barrier(jnp.sum(expo, axis=2)) + jnp.exp(outside.T - highest)
    return lax.optimization_barrier(jnp.sum(expo / total[:, :, None], axis=0))

def score_grad(mass, index_score, visible, outside):
    target = mass / lax.optimization_barrier(jnp.sum(mass, axis=1, keepdims=True))
    masked = jnp.where(visible, index_score, NEGATIVE)
    highest = jnp.maximum(lax.optimization_barrier(jnp.max(masked, axis=1)), outside)
    expo = jnp.exp(masked - highest[:, None])
    total = lax.optimization_barrier(jnp.sum(expo, axis=1)) + jnp.exp(outside - highest)
    return (expo / total[:, None] - target) * (STEPS * KB)

def reference(main_query, latent, main_outside, index_query, index_weights, index_keys, index_outside, query_pos, key_pos):
    window = STEPS * KB
    front = (STEPS - 1) * KB
    latent_padded = jnp.concatenate([jnp.zeros((front, LAT + ROPE), latent.dtype), latent], 0)
    keys_padded = jnp.concatenate([jnp.zeros((front, IDIM), index_keys.dtype), index_keys], 0)
    places_padded = jnp.concatenate([jnp.zeros((front,), jnp.int32), key_pos.astype(jnp.int32)], 0)
    factor = IDIM ** (-0.5)
    slot_block = (jnp.arange(window, dtype=jnp.int32) // KB).astype(jnp.int32)
    lagging = (STEPS - 1 - slot_block).astype(jnp.int32)

    def one_block(grad_keys, block_index):
        first = (block_index * Q_DEV).astype(jnp.int32)
        key_first = (block_index * KB).astype(jnp.int32)
        queries = lax.dynamic_slice_in_dim(main_query, first, Q_DEV, 0).reshape(Q_DEV, HEADS, LAT + ROPE).astype(jnp.float32)
        latent_window = lax.dynamic_slice_in_dim(latent_padded, key_first, window, 0).astype(jnp.float32)
        key_window = lax.dynamic_slice_in_dim(keys_padded, key_first, window, 0)
        place_window = lax.dynamic_slice_in_dim(places_padded, key_first, window, 0)
        outside = lax.dynamic_slice_in_dim(main_outside, first, Q_DEV, 0)
        index_out = lax.dynamic_slice_in_dim(index_outside, first, Q_DEV, 0)
        query_places = lax.dynamic_slice_in_dim(query_pos.astype(jnp.int32), first, Q_DEV, 0)
        index_rows = lax.dynamic_slice_in_dim(index_query, first, Q_DEV, 0).reshape(Q_DEV, IHEADS, IDIM).astype(jnp.float32)
        weight_rows = lax.dynamic_slice_in_dim(index_weights, first, Q_DEV, 0)
        causal = (slot_block < STEPS - 1)[None, :] | (place_window[None, :] <= query_places[:, None])
        visible = (block_index >= lagging)[None, :] & causal
        scores = jnp.einsum('qhc,wc->hqw', queries, latent_window) * SCORE_SCALE
        mass = head_mass(scores, visible, outside)
        key_wide = key_window.astype(jnp.float32)
        activity = jnp.einsum('qjd,wd->jqw', index_rows, key_wide) * factor
        rectified = jnp.maximum(activity, 0.0)
        index_score = jnp.einsum('qj,jqw->qw', weight_rows, rectified)
        dscore = score_grad(mass, index_score, visible, index_out)
        gated = dscore[None] * weight_rows.T[:, :, None] * (activity > 0).astype(jnp.float32)
        grad_query = (jnp.einsum('jqw,wd->qjd', gated, key_wide, precision=lax.Precision.HIGHEST) * factor).astype(jnp.bfloat16)
        grad_weight = jnp.einsum('qw,jqw->qj', dscore, rectified)
        grad_key = jnp.einsum('jqw,qjd->wd', gated, index_rows, precision=lax.Precision.HIGHEST) * factor
        current = lax.dynamic_slice_in_dim(grad_keys, key_first, window, 0)
        grad_keys = lax.dynamic_update_slice_in_dim(grad_keys, current + grad_key, key_first, 0)
        return (grad_keys, (grad_query.reshape(Q_DEV, IHEADS * IDIM), grad_weight))
    start_keys = jnp.zeros((front + KEYS, IDIM), jnp.float32)
    grad_keys, stacked = lax.scan(one_block, start_keys, jnp.arange(N_SEQ, dtype=jnp.int32))
    grad_query = stacked[0].reshape(QUERIES, IHEADS * IDIM)
    grad_weight = stacked[1].reshape(QUERIES, IHEADS)
    return (grad_query, grad_weight, grad_keys[front:])
```

```python
import functools

import jax
import jax.numpy as jnp
from jax import lax
from jax.experimental import pallas as pl
from jax.experimental.pallas import tpu as pltpu
from jax.sharding import PartitionSpec as P

IDIM = 128
KB = 256
STEPS = 4


NEGATIVE = -1e30
SCORE_SCALE = 192.0 ** (-0.5)


def passed_along(block, axis, distance):
    devices = range(lax.axis_size(axis))
    route = [(i - distance, i) for i in devices if i - distance in devices]
    return lax.ppermute(block, axis, route)


def head_mass(scores, visible, outside):
    masked = jnp.where(visible[None], scores, NEGATIVE)
    highest = jnp.maximum(jnp.max(masked, axis=2), outside.T)
    expo = jnp.exp(masked - highest[:, :, None])
    total = jnp.sum(expo, axis=2) + jnp.exp(outside.T - highest)
    return jnp.sum(expo / total[:, :, None], axis=0)


def score_grad(mass, index_score, visible, outside):
    target = mass / jnp.sum(mass, axis=1, keepdims=True)
    masked = jnp.where(visible, index_score, NEGATIVE)
    highest = jnp.maximum(jnp.max(masked, axis=1), outside)
    expo = jnp.exp(masked - highest[:, None])
    total = jnp.sum(expo, axis=1) + jnp.exp(outside - highest)
    return (expo / total[:, None] - target) * (STEPS * KB)


def plain_shards(
    main_query,
    latent,
    main_outside,
    index_query,
    index_weights,
    index_keys,
    index_outside,
    query_pos,
    key_pos,
):
    query_rows = main_query.shape[0]
    block_keys = latent.shape[0]
    width = latent.shape[1]
    local_heads = main_outside.shape[1]
    local_index = index_weights.shape[1]
    index_width = index_keys.shape[1]
    window = STEPS * block_keys
    factor = IDIM ** (-0.5)
    position = lax.axis_index("seq")
    latent_parts = []
    index_parts = []
    for distance in range(STEPS - 1, 0, -1):
        latent_parts.append(passed_along(latent, "seq", distance))
        index_parts.append(passed_along(index_keys, "seq", distance))
    latent_window = jnp.concatenate(latent_parts + [latent], 0)
    key_window = jnp.concatenate(index_parts + [index_keys], 0)
    slot_block = jnp.arange(window, dtype=jnp.int32) // block_keys
    lagging = STEPS - 1 - slot_block
    places_full = jnp.concatenate([jnp.zeros((window - block_keys,), jnp.int32), key_pos], 0)
    causal = (slot_block < STEPS - 1)[None, :] | (places_full[None, :] <= query_pos[:, None])
    visible = (position >= lagging)[None, :] & causal
    queries = main_query.reshape(query_rows, local_heads, width)
    scores = (
        jnp.einsum("qhc,wc->hqw", queries, latent_window, preferred_element_type=jnp.float32)
        * SCORE_SCALE
    )
    mass_part = head_mass(scores, visible, main_outside)
    index_rows = index_query.reshape(query_rows, local_index, index_width)
    activity = (
        jnp.einsum("qjd,wd->jqw", index_rows, key_window, preferred_element_type=jnp.float32)
        * factor
    )
    rectified = jnp.maximum(activity, 0.0)
    index_part = jnp.einsum("qj,jqw->qw", index_weights, rectified)
    mass, index_score = (
        lax.psum_scatter(mass_part, "head", scatter_dimension=0, tiled=True),
        lax.psum_scatter(index_part, "head", scatter_dimension=0, tiled=True),
    )
    share = mass.shape[0]
    start = lax.axis_index("head") * share
    visible_rows = lax.dynamic_slice_in_dim(visible, start, share, 0)
    outside_rows = lax.dynamic_slice_in_dim(index_outside, start, share, 0)
    dscore = lax.all_gather(
        score_grad(mass, index_score, visible_rows, outside_rows), "head", axis=0, tiled=True
    )
    gated = dscore[None] * index_weights.T[:, :, None] * (activity > 0).astype(jnp.float32)
    key_wide = key_window.astype(jnp.float32)
    rows_wide = index_rows.astype(jnp.float32)
    grad_query = (
        jnp.einsum("jqw,wd->qjd", gated, key_wide, precision=lax.Precision.HIGHEST) * factor
    )
    grad_query = grad_query.astype(jnp.bfloat16).reshape(query_rows, local_index * index_width)
    grad_weight = jnp.einsum("qw,jqw->qj", dscore, rectified)
    grad_window = (
        jnp.einsum("jqw,qjd->wd", gated, rows_wide, precision=lax.Precision.HIGHEST) * factor
    )
    grad_parts = grad_window.reshape(STEPS, block_keys, index_width)
    grad_total = grad_parts[STEPS - 1]
    for distance in range(1, STEPS):
        grad_total = grad_total + passed_along(grad_parts[STEPS - 1 - distance], "seq", -distance)
    grad_keys = lax.psum(grad_total, "head")
    return (grad_query, grad_weight, grad_keys)


LOG2E = 1.4426950408889634
LAT = 576
PACK = 768
GROUPS = 4
SAFE = 1e30
NT = (((1,), (1,)), ((), ()))


def dot(a, b, dims=(((1,), (0,)), ((), ()))):
    return lax.dot_general(a, b, dims, preferred_element_type=jnp.float32)


def slots_of(even):
    return jnp.where(even, 0, 2), jnp.where(even, 2, 0)


def main_kernel(heads, place, q, own, a, b, c, outside, qpos, kpos, *rest):
    outs, (k_even, k_odd, e, inv, out_exp, mass) = rest[:GROUPS], rest[GROUPS:]
    step, steps = pl.program_id(0), pl.num_programs(0)
    z, position = place[0], place[1]
    rows, kb = q.shape[0], own.shape[0]
    half = heads // 2
    window = STEPS * kb
    present = [jnp.where(position >= STEPS - 1 - i, 1.0, 0.0).astype(jnp.float32) for i in range(STEPS)]
    now = lax.rem(step, 2)

    @pl.when(step == 0)
    def _():
        slot_a, slot_b = slots_of(lax.rem(position, 2) == 0)
        zeros = jnp.zeros((kb, 64), jnp.bfloat16)
        for block, slot in ((own, 3), (a, slot_a), (b, slot_b), (c, 1)):
            at = pl.ds(pl.multiple_of(slot * kb, kb), kb)
            k_even[at, :] = block[:, :640]
            k_odd[at, :] = jnp.concatenate([zeros, block[:, :LAT]], 1)
        mass[...] = jnp.zeros_like(mass)
        lanes = jnp.concatenate([outside[...], jnp.full((rows, 128 - outside.shape[1]), NEGATIVE, jnp.float32)], 1)
        out_exp[...] = jnp.exp(lanes)

    def add_mass(buffer):
        for r in range(0, rows, 32):
            for w in range(0, window, 256):
                total = mass[r:r + 32, w:w + 256]
                for h in range(heads):
                    scale = inv[buffer, h * rows + r:h * rows + r + 32, :]
                    part = e[buffer, h * rows + r:h * rows + r + 32, w:w + 256]
                    total = total + part * jnp.concatenate([scale, scale], 1)
                mass[r:r + 32, w:w + 256] = total

    @pl.when(step > 0)
    def _():
        add_mass(1 - now)

    lane = lax.broadcasted_iota(jnp.int32, (32, 128), 1)
    worst = jnp.zeros((32, 1), jnp.float32)
    for parity, keys in ((0, k_even), (1, k_odd)):
        lhs = jnp.concatenate([q[:, 1152 * i + 512 * parity:1152 * i + 512 * parity + 640] for i in range(half)], 0)
        base = parity * half * rows
        e[now, base:base + half * rows, :] = dot(lhs, keys[...], NT)
    for parity in range(2):
        for i in range(half):
            for r in range(0, rows, 32):
                at = (parity * half + i) * rows + r
                ex = jnp.exp2(e[now, at:at + 32, :] * (SCORE_SCALE * LOG2E))
                causal = kpos[...] <= qpos[r:r + 32, :]
                last = jnp.where(causal, ex[:, window - kb:], 0.0)
                head = step * heads + 2 * i + parity
                total = jnp.where(lane == head, out_exp[r:r + 32, :], 0.0)
                for block in range(STEPS):
                    piece = last if block == STEPS - 1 else ex[:, block * kb:(block + 1) * kb]
                    e[now, at:at + 32, block * kb:(block + 1) * kb] = piece
                    lanes = piece[:, :128]
                    for k in range(128, kb, 128):
                        lanes = lanes + piece[:, k:k + 128]
                    total = total + (lanes if block == STEPS - 1 else lanes * present[block])
                total = jnp.sum(total, axis=1, keepdims=True)
                worst = jnp.maximum(worst, total)
                inv[now, at:at + 32, :] = jnp.broadcast_to(1.0 / total, (32, 128))

    @pl.when(jnp.logical_not(jnp.max(worst) < SAFE))
    def _():
        slot = lax.broadcasted_iota(jnp.int32, (rows, window), 1) // kb
        causal = jnp.concatenate([jnp.ones((rows, window - kb), jnp.bool_), kpos[...] <= qpos[...]], 1)
        visible = (position >= STEPS - 1 - slot) & causal
        wide = lax.broadcasted_iota(jnp.int32, (rows, 32), 1)
        for parity, keys in ((0, k_even), (1, k_odd)):

            def exact(i, carry, parity=parity, keys=keys):
                at = pl.multiple_of(1152 * i + 512 * parity, 128)
                scores = dot(q[:, pl.ds(at, 640)], keys[...], NT) * SCORE_SCALE
                masked = jnp.where(visible, scores, NEGATIVE)
                head = step * heads + 2 * i + parity
                mine = jnp.sum(jnp.where(wide == head, outside[...], 0.0), axis=1, keepdims=True)
                top = jnp.maximum(jnp.max(masked, axis=1, keepdims=True), mine)
                ex = jnp.exp(masked - top)
                total = jnp.sum(ex, axis=1, keepdims=True) + jnp.exp(mine - top)
                row = pl.ds(pl.multiple_of((parity * half + i) * rows, rows), rows)
                e[now, row, :] = ex
                inv[now, row, :] = jnp.broadcast_to(1.0 / total, (rows, 128))
                return carry

            lax.fori_loop(0, half, exact, 0)

    @pl.when(step == steps - 1)
    def _():
        add_mass(now)
        share = rows // GROUPS
        for d in range(GROUPS):
            at = pl.ds(pl.multiple_of((z ^ d) * share, share), share)
            for block in range(STEPS):
                lanes = slice(block * kb, (block + 1) * kb)
                outs[d][:, lanes] = mass[at, lanes] * present[block]


def gathered_keys(place, blocks, keys):
    own, a, b, c = blocks
    kb = own.shape[0]
    slot_a, slot_b = slots_of(lax.rem(place[1], 2) == 0)
    for block, slot in ((own, 3), (a, slot_a), (b, slot_b), (c, 1)):
        keys[pl.ds(pl.multiple_of(slot * kb, kb), kb), :] = block[...]


def weights_of(piece, width, count):
    tail = piece[:, width:].astype(jnp.float32)
    return tail[:, :count] + tail[:, count:2 * count] + tail[:, 2 * count:3 * count]


def heads_of(piece, count):
    return jnp.concatenate([piece[:, IDIM * j:IDIM * (j + 1)] for j in range(count)], 0)


def index_kernel(count, place, own, a, b, c, *rest):
    pieces, (score, gate, turned), (keys, every) = rest[:GROUPS], rest[GROUPS:GROUPS + 3], rest[GROUPS + 3:]
    step = pl.program_id(0)
    share = score.shape[0]

    @pl.when(step == 0)
    def _():
        gathered_keys(place, (own, a, b, c), keys)
        for d in range(GROUPS):
            every[d] = pieces[d][...]
        score[...] = jnp.zeros_like(score)

    piece = every[step]
    weight = weights_of(piece, IDIM * count, count)
    rows = heads_of(piece, count)
    act = dot(rows, keys[...], NT)
    gate[...] = jnp.where(act > 0, 1.0, 0.0).astype(jnp.bfloat16)
    scaled = weight * (IDIM ** -0.5)
    total = score[...]
    for j in range(count):
        total = total + jnp.maximum(act[j * share:(j + 1) * share], 0.0) * scaled[:, j:j + 1]
    score[...] = total
    tall = jnp.concatenate([jnp.broadcast_to(scaled[:, j:j + 1], (share, IDIM)) for j in range(count)], 0)
    weighted = rows.astype(jnp.float32) * tall
    high = weighted.astype(jnp.bfloat16)
    low = (weighted - high.astype(jnp.float32)).astype(jnp.bfloat16)
    turned[:IDIM, :] = high.T
    turned[IDIM:, :] = low.T


def split(x):
    high = x.astype(jnp.bfloat16)
    return high, (x - high.astype(jnp.float32)).astype(jnp.bfloat16)


def query_kernel(count, place, own, a, b, c, m0, m1, m2, m3, score, outside, qpos, kpos, gate, *rest):
    pieces, outs, spread = rest[:GROUPS], rest[GROUPS:2 * GROUPS], rest[2 * GROUPS]
    keys, every, back = rest[2 * GROUPS + 1:]
    step, steps = pl.program_id(0), pl.num_programs(0)
    position = place[1]
    share, window = score.shape
    kb = own.shape[0]

    @pl.when(step == 0)
    def _():
        gathered_keys(place, (own, a, b, c), keys)
        for d in range(GROUPS):
            every[d] = pieces[d][...]
        mass = (m0[...] + m1[...]) + (m2[...] + m3[...])
        target = mass / jnp.sum(mass, axis=1, keepdims=True)
        mine = pl.ds(pl.multiple_of(place[0] * share, share), share)
        slot = lax.broadcasted_iota(jnp.int32, (share, window), 1) // kb
        causal = kpos[...] <= qpos[mine, :]
        masked = jnp.where(position >= STEPS - 1 - slot, score[...], NEGATIVE)
        masked = jnp.concatenate([masked[:, :window - kb], jnp.where(causal, masked[:, window - kb:], NEGATIVE)], 1)
        out = outside[mine, :]
        top = jnp.maximum(jnp.max(masked, axis=1, keepdims=True), out)
        expo = jnp.exp(masked - top)
        total = jnp.sum(expo, axis=1, keepdims=True) + jnp.exp(out - top)
        dscore = (expo / total - target) * float(window)
        high, low = split(dscore)
        spread[0] = high
        spread[1] = low

    piece = every[step]
    weight = weights_of(piece, IDIM * count, count)
    mask = gate[...]
    grad = dot(mask * jnp.concatenate([spread[0]] * count, 0), keys[...])
    grad = grad + dot(mask * jnp.concatenate([spread[1]] * count, 0), keys[...])
    lane = lax.broadcasted_iota(jnp.int32, (share, 128), 1)
    sums = jnp.zeros((share, 128), jnp.float32)
    factor = IDIM ** -0.5
    for j in range(count):
        mine = grad[j * share:(j + 1) * share] * factor
        lanes = slice(IDIM * j, IDIM * (j + 1))
        back[step, :, lanes] = (mine * weight[:, j:j + 1]).astype(jnp.bfloat16)
        product = jnp.sum(mine * piece[:, lanes].astype(jnp.float32), axis=1, keepdims=True)
        sums = jnp.where(lane == j, product, sums)
    sums = sums[:, :count]
    high = sums.astype(jnp.bfloat16)
    left = sums - high.astype(jnp.float32)
    middle = left.astype(jnp.bfloat16)
    low = (left - middle.astype(jnp.float32)).astype(jnp.bfloat16)
    tail = jnp.concatenate([high, middle, low, jnp.zeros((share, 128 - 3 * count), jnp.bfloat16)], 1)
    back[step, :, IDIM * count:] = tail

    @pl.when(step == steps - 1)
    def _():
        for d in range(GROUPS):
            outs[d][...] = back[d]


def keys_kernel(count, gate, turned, spread, *rest):
    outs, total = rest[:STEPS], rest[STEPS]
    step, steps = pl.program_id(0), pl.num_programs(0)

    @pl.when(step == 0)
    def _():
        total[...] = jnp.zeros_like(total)

    mask = gate[...]
    both = dot(turned[...], mask * jnp.concatenate([spread[0]] * count, 0))
    low = dot(turned[:IDIM, :], mask * jnp.concatenate([spread[1]] * count, 0))
    total[...] += both[:IDIM] + both[IDIM:] + low

    @pl.when(step == steps - 1)
    def _():
        kb = outs[0].shape[0]
        for i in range(STEPS):
            outs[i][...] = total[:, i * kb:(i + 1) * kb].T


def place_kernel(count, place, *rest):
    pieces, (grad, weight) = rest[:GROUPS], rest[GROUPS:]
    share = pieces[0].shape[0]
    for d in range(GROUPS):
        at = pl.ds(pl.multiple_of((place[0] ^ d) * share, share), share)
        grad[at, :] = pieces[d][:, :IDIM * count]
        weight[at, :] = weights_of(pieces[d][...], IDIM * count, count)


SMEM = pl.BlockSpec(memory_space=pltpu.SMEM)


def whole(array):
    rank = len(array.shape)
    return pl.BlockSpec(array.shape, lambda i: (0,) * rank)


def params(mib):
    return pltpu.CompilerParams(vmem_limit_bytes=mib << 20)


def along(x, axis, route):
    return lax.ppermute(x, axis, [(i, j) for i, j in route if 0 <= j < lax.axis_size(axis)])


def shards(
    main_query,
    latent,
    main_outside,
    index_query,
    index_weights,
    index_keys,
    index_outside,
    query_pos,
    key_pos,
):
    rows = main_query.shape[0]
    kb = latent.shape[0]
    heads = main_outside.shape[1]
    count = index_weights.shape[1]
    share = rows // GROUPS
    window = STEPS * kb
    n_seq = lax.axis_size("seq")
    z, position = lax.axis_index("head"), lax.axis_index("seq")
    place = jnp.stack([z, position]).astype(jnp.int32)
    bf16, f32 = jnp.bfloat16, jnp.float32

    packed = jnp.concatenate([latent, jnp.zeros((kb, PACK - LAT - IDIM), bf16), index_keys], 1)
    route_b = along(packed, "seq", [(i, i + (3 if i % 2 == 0 else 1)) for i in range(n_seq)])
    route_a = along(packed, "seq", [(i, i + (1 if i % 2 == 0 else 3)) for i in range(n_seq)])
    route_c = along(route_b, "seq", [(i, i ^ 1) for i in range(n_seq)])
    blocks = (packed, route_a, route_b, route_c)

    high = lax.reduce_precision(index_weights, 8, 7)
    middle = lax.reduce_precision(index_weights - high, 8, 7)
    low = index_weights - high - middle
    tail = jnp.concatenate([high, middle, low, jnp.zeros((rows, 128 - 3 * count), f32)], 1)
    rows_packed = jnp.concatenate([index_query, tail.astype(bf16)], 1)

    def exchanged(x, d):
        return along(x, "head", [(i, i ^ d) for i in range(GROUPS)])

    mine = [lax.dynamic_slice_in_dim(rows_packed, (z ^ d) * share, share, 0) for d in range(GROUPS)]
    pieces = [mine[0]] + [exchanged(mine[d], d) for d in range(1, GROUPS)]

    qpos = query_pos.reshape(rows, 1)
    kpos = key_pos.reshape(1, kb)
    outside = index_outside.reshape(rows, 1)

    per_step = 8
    mass = pl.pallas_call(
        functools.partial(main_kernel, per_step),
        grid=(heads // per_step,),
        in_specs=[SMEM, pl.BlockSpec((rows, per_step * LAT), lambda i: (0, i))]
        + [whole(x) for x in blocks]
        + [whole(main_outside), whole(qpos), whole(kpos)],
        out_specs=[pl.BlockSpec((share, window), lambda i: (0, 0))] * GROUPS,
        out_shape=[jax.ShapeDtypeStruct((share, window), f32)] * GROUPS,
        scratch_shapes=[
            pltpu.VMEM((window, 640), bf16),
            pltpu.VMEM((window, 640), bf16),
            pltpu.VMEM((2, per_step * rows, window), f32),
            pltpu.VMEM((2, per_step * rows, 128), f32),
            pltpu.VMEM((rows, 128), f32),
            pltpu.VMEM((rows, window), f32),
        ],
        compiler_params=params(48),
        name="main_mass",
    )(place, main_query, *blocks, main_outside, qpos, kpos)
    masses = [mass[0]] + [exchanged(mass[d], d) for d in range(1, GROUPS)]

    tile = count * share
    key_spec = pl.BlockSpec((kb, IDIM), lambda i: (0, PACK // IDIM - 1))
    piece_shape = (share, IDIM * count + 128)
    score, gate, turned = pl.pallas_call(
        functools.partial(index_kernel, count),
        grid=(GROUPS,),
        in_specs=[SMEM] + [key_spec] * 4 + [whole(x) for x in pieces],
        out_specs=[
            pl.BlockSpec((share, window), lambda i: (0, 0)),
            pl.BlockSpec((tile, window), lambda i: (i, 0)),
            pl.BlockSpec((2 * IDIM, tile), lambda i: (0, i)),
        ],
        out_shape=[
            jax.ShapeDtypeStruct((share, window), f32),
            jax.ShapeDtypeStruct((GROUPS * tile, window), bf16),
            jax.ShapeDtypeStruct((2 * IDIM, GROUPS * tile), bf16),
        ],
        scratch_shapes=[pltpu.VMEM((window, IDIM), bf16), pltpu.VMEM((GROUPS,) + piece_shape, bf16)],
        compiler_params=params(32),
        name="index_scores",
    )(place, *blocks, *pieces)

    *back, spread = pl.pallas_call(
        functools.partial(query_kernel, count),
        grid=(GROUPS,),
        in_specs=[SMEM] + [key_spec] * 4 + [whole(x) for x in masses]
        + [whole(score), whole(outside), whole(qpos), whole(kpos)]
        + [pl.BlockSpec((tile, window), lambda i: (i, 0))]
        + [whole(x) for x in pieces],
        out_specs=[pl.BlockSpec(piece_shape, lambda i: (0, 0))] * GROUPS
        + [pl.BlockSpec((2, share, window), lambda i: (0, 0, 0))],
        out_shape=[jax.ShapeDtypeStruct(piece_shape, bf16)] * GROUPS
        + [jax.ShapeDtypeStruct((2, share, window), bf16)],
        scratch_shapes=[
            pltpu.VMEM((window, IDIM), bf16),
            pltpu.VMEM((GROUPS,) + piece_shape, bf16),
            pltpu.VMEM((GROUPS,) + piece_shape, bf16),
        ],
        compiler_params=params(32),
        name="query_grads",
    )(place, *blocks, *masses, score, outside, qpos, kpos, gate, *pieces)
    returned = [back[0]] + [exchanged(back[d], d) for d in range(1, GROUPS)]

    parts = pl.pallas_call(
        functools.partial(keys_kernel, count),
        grid=(GROUPS,),
        in_specs=[
            pl.BlockSpec((tile, window), lambda i: (i, 0)),
            pl.BlockSpec((2 * IDIM, tile), lambda i: (0, i)),
            whole(spread),
        ],
        out_specs=[pl.BlockSpec((kb, IDIM), lambda i: (0, 0))] * STEPS,
        out_shape=[jax.ShapeDtypeStruct((kb, IDIM), f32)] * STEPS,
        scratch_shapes=[pltpu.VMEM((IDIM, window), f32)],
        compiler_params=params(32),
        name="key_grads",
    )(gate, turned, spread)
    owned = parts[STEPS - 1]
    for distance in range(1, STEPS):
        owned = owned + along(parts[STEPS - 1 - distance], "seq", [(i, i - distance) for i in range(n_seq)])
    others = [exchanged(owned, d) for d in range(1, GROUPS)]
    grad_keys = (owned + others[0]) + (others[1] + others[2])

    grad_query, grad_weight = pl.pallas_call(
        functools.partial(place_kernel, count),
        grid=(1,),
        in_specs=[SMEM] + [whole(x) for x in returned],
        out_specs=[
            pl.BlockSpec((rows, IDIM * count), lambda i: (0, 0)),
            pl.BlockSpec((rows, count), lambda i: (0, 0)),
        ],
        out_shape=[
            jax.ShapeDtypeStruct((rows, IDIM * count), bf16),
            jax.ShapeDtypeStruct((rows, count), f32),
        ],
        compiler_params=params(32),
        name="place_grads",
    )(place, *returned)
    return (grad_query, grad_weight, grad_keys)


def any_shards(main_query, latent, main_outside, index_query, index_weights, index_keys, *rest):
    args = (main_query, latent, main_outside, index_query, index_weights, index_keys, *rest)
    fits = (
        lax.axis_size("head") == GROUPS
        and lax.axis_size("seq") % 2 == 0
        and main_query.shape[0] % (32 * GROUPS) == 0
        and main_outside.shape[1] % 8 == 0
        and latent.shape[0] % 256 == 0
        and latent.shape[1] == LAT
        and 3 * index_weights.shape[1] <= 128
    )
    return shards(*args) if fits else plain_shards(*args)


def solution(mesh):
    in_specs = (
        P("seq", "head"),
        P("seq", None),
        P("seq", "head"),
        P("seq", "head"),
        P("seq", "head"),
        P("seq", None),
        P("seq"),
        P("seq"),
        P("seq"),
    )
    out_specs = (P("seq", "head"), P("seq", "head"), P("seq", None))
    return jax.shard_map(any_shards, mesh=mesh, in_specs=in_specs, out_specs=out_specs, check_vma=False)
```

```python
import functools

import jax
import jax.numpy as jnp
from jax import lax
from jax.experimental import pallas as pl
from jax.experimental.pallas import tpu as pltpu
from jax.sharding import PartitionSpec as P

IDIM = 128
KB = 256
STEPS = 4


NEGATIVE = -1e30
SCORE_SCALE = 192.0 ** (-0.5)


def passed_along(block, axis, distance):
    devices = range(lax.axis_size(axis))
    route = [(i - distance, i) for i in devices if i - distance in devices]
    return lax.ppermute(block, axis, route)


def head_mass(scores, visible, outside):
    masked = jnp.where(visible[None], scores, NEGATIVE)
    highest = jnp.maximum(jnp.max(masked, axis=2), outside.T)
    expo = jnp.exp(masked - highest[:, :, None])
    total = jnp.sum(expo, axis=2) + jnp.exp(outside.T - highest)
    return jnp.sum(expo / total[:, :, None], axis=0)


def score_grad(mass, index_score, visible, outside):
    target = mass / jnp.sum(mass, axis=1, keepdims=True)
    masked = jnp.where(visible, index_score, NEGATIVE)
    highest = jnp.maximum(jnp.max(masked, axis=1), outside)
    expo = jnp.exp(masked - highest[:, None])
    total = jnp.sum(expo, axis=1) + jnp.exp(outside - highest)
    return (expo / total[:, None] - target) * (STEPS * KB)


def plain_shards(
    main_query,
    latent,
    main_outside,
    index_query,
    index_weights,
    index_keys,
    index_outside,
    query_pos,
    key_pos,
):
    query_rows = main_query.shape[0]
    block_keys = latent.shape[0]
    width = latent.shape[1]
    local_heads = main_outside.shape[1]
    local_index = index_weights.shape[1]
    index_width = index_keys.shape[1]
    window = STEPS * block_keys
    factor = IDIM ** (-0.5)
    position = lax.axis_index("seq")
    latent_parts = []
    index_parts = []
    for distance in range(STEPS - 1, 0, -1):
        latent_parts.append(passed_along(latent, "seq", distance))
        index_parts.append(passed_along(index_keys, "seq", distance))
    latent_window = jnp.concatenate(latent_parts + [latent], 0)
    key_window = jnp.concatenate(index_parts + [index_keys], 0)
    slot_block = jnp.arange(window, dtype=jnp.int32) // block_keys
    lagging = STEPS - 1 - slot_block
    places_full = jnp.concatenate([jnp.zeros((window - block_keys,), jnp.int32), key_pos], 0)
    causal = (slot_block < STEPS - 1)[None, :] | (places_full[None, :] <= query_pos[:, None])
    visible = (position >= lagging)[None, :] & causal
    queries = main_query.reshape(query_rows, local_heads, width)
    scores = (
        jnp.einsum("qhc,wc->hqw", queries, latent_window, preferred_element_type=jnp.float32)
        * SCORE_SCALE
    )
    mass_part = head_mass(scores, visible, main_outside)
    index_rows = index_query.reshape(query_rows, local_index, index_width)
    activity = (
        jnp.einsum("qjd,wd->jqw", index_rows, key_window, preferred_element_type=jnp.float32)
        * factor
    )
    rectified = jnp.maximum(activity, 0.0)
    index_part = jnp.einsum("qj,jqw->qw", index_weights, rectified)
    mass, index_score = (
        lax.psum_scatter(mass_part, "head", scatter_dimension=0, tiled=True),
        lax.psum_scatter(index_part, "head", scatter_dimension=0, tiled=True),
    )
    share = mass.shape[0]
    start = lax.axis_index("head") * share
    visible_rows = lax.dynamic_slice_in_dim(visible, start, share, 0)
    outside_rows = lax.dynamic_slice_in_dim(index_outside, start, share, 0)
    dscore = lax.all_gather(
        score_grad(mass, index_score, visible_rows, outside_rows), "head", axis=0, tiled=True
    )
    gated = dscore[None] * index_weights.T[:, :, None] * (activity > 0).astype(jnp.float32)
    key_wide = key_window.astype(jnp.float32)
    rows_wide = index_rows.astype(jnp.float32)
    grad_query = (
        jnp.einsum("jqw,wd->qjd", gated, key_wide, precision=lax.Precision.HIGHEST) * factor
    )
    grad_query = grad_query.astype(jnp.bfloat16).reshape(query_rows, local_index * index_width)
    grad_weight = jnp.einsum("qw,jqw->qj", dscore, rectified)
    grad_window = (
        jnp.einsum("jqw,qjd->wd", gated, rows_wide, precision=lax.Precision.HIGHEST) * factor
    )
    grad_parts = grad_window.reshape(STEPS, block_keys, index_width)
    grad_total = grad_parts[STEPS - 1]
    for distance in range(1, STEPS):
        grad_total = grad_total + passed_along(grad_parts[STEPS - 1 - distance], "seq", -distance)
    grad_keys = lax.psum(grad_total, "head")
    return (grad_query, grad_weight, grad_keys)


LOG2E = 1.4426950408889634
LAT = 576
GROUPS = 4
BUFFERS = 4
PER_STEP = 8
SAFE = 1e30
LEVELS = 32000.0
NN = (((1,), (0,)), ((), ()))
NT = (((1,), (1,)), ((), ()))


def dot(a, b, dims=NN):
    return lax.dot_general(a, b, dims, preferred_element_type=jnp.float32)


def split(x):
    high = x.astype(jnp.bfloat16)
    return high, (x - high.astype(jnp.float32)).astype(jnp.bfloat16)


def coded(x, axis):
    top = jnp.max(jnp.abs(x), axis=axis, keepdims=True)
    power = jnp.ceil(8.0 * jnp.log2(jnp.maximum(top, 1e-30)))
    code = jnp.floor(x * (LEVELS * jnp.exp2(power * -0.125)) + 0.5)
    return code.astype(jnp.int32).astype(jnp.int16), power.astype(jnp.int32).astype(jnp.int16)


def scale_of(power):
    return jnp.exp2(power.astype(jnp.float32) * 0.125) * (1.0 / LEVELS)


def coded_rows(ref, x):
    code, power = coded(x, 1)
    ref[:, :x.shape[1]] = code
    ref[:, x.shape[1]:] = jnp.broadcast_to(power.astype(jnp.int32), (x.shape[0], 128)).astype(jnp.int16)


def restored_rows(ref, window):
    return ref[:, :window].astype(jnp.float32) * scale_of(ref[:, window:])[:, :1]


def coded_columns(ref, x):
    code, power = coded(x, 0)
    ref[:x.shape[0], :] = code
    ref[x.shape[0]:, :] = jnp.broadcast_to(power.astype(jnp.int32), (16, x.shape[1])).astype(jnp.int16)


def restored_columns(ref, count):
    return ref[:count, :].astype(jnp.float32) * scale_of(ref[count:, :])[:1, :]


def column(row, first, count):
    lane = lax.broadcasted_iota(jnp.int32, (count, 128), 1)
    line = lax.broadcasted_iota(jnp.int32, (count, 128), 0) + first
    wide = jnp.broadcast_to(row.astype(jnp.float32), (count, 128))
    return jnp.sum(jnp.where(lane == line, wide, 0.0), axis=1, keepdims=True)


def turned_tall(x, value=0.0):
    fill = jnp.full((128 - x.shape[0], 128), value, jnp.float32)
    return jnp.concatenate([x, fill], 0).T


def slots_of(position):
    even = lax.rem(position, 2) == 0
    return 3, jnp.where(even, 0, 2), jnp.where(even, 2, 0), 1


def gathered(position, blocks, kept, first):
    kb = blocks[0].shape[1]
    for block, slot in zip(blocks, slots_of(position)):
        at = pl.ds(pl.multiple_of(slot * kb, kb), kb)
        kept[first:first + block.shape[0], at] = block[...]


def heads_at(q, parity):
    starts = [1152 * i + 512 * parity for i in range(q.shape[1] // 1152)]
    return jnp.concatenate([q[:, s:s + 640] for s in starts], 0)


def pack_kernel(place, latent, keys, query, weight, packed, *rest):
    outs, (kept, keys_here, weight_here, sems) = rest[:GROUPS], rest[GROUPS:]
    share = outs[0].shape[0]
    width, count = query.shape[1], weight.shape[0]
    copies = [
        pltpu.make_async_copy(latent, packed.at[pl.ds(0, LAT), :], sems.at[0]),
        pltpu.make_async_copy(keys, keys_here, sems.at[1]),
        pltpu.make_async_copy(weight, weight_here, sems.at[2]),
    ]
    for d in range(GROUPS):
        at = pl.ds(pl.multiple_of((place[0] ^ d) * share, share), share)
        here = outs[d].at[:, pl.ds(0, width)]
        copies.append(pltpu.make_async_copy(query.at[at, :], here, sems.at[3 + d]))
    for copy in copies:
        copy.start()
    copies[1].wait()
    packed[LAT:, :] = keys_here[...].T
    copies[2].wait()
    tall = turned_tall(weight_here[...])[:, :count]
    high = tall.astype(jnp.bfloat16)
    middle, low = split(tall - high.astype(jnp.float32))
    kept[...] = jnp.concatenate([high, middle, low, jnp.zeros((128, 128 - 3 * count), jnp.bfloat16)], 1)
    for d in range(GROUPS):
        at = pl.ds(pl.multiple_of((place[0] ^ d) * share, share), share)
        outs[d][:, width:] = kept[at, :]
    copies[0].wait()
    for copy in copies[3:]:
        copy.wait()


def weights_of(piece, width, count):
    tail = piece[:, width:].astype(jnp.float32)
    return tail[:, :count] + tail[:, count:2 * count] + tail[:, 2 * count:3 * count]


def chunk_rows(q, j, half):
    parity, pair = j % 2, half * (j // 2)
    starts = [1152 * (pair + i) + 512 * parity for i in range(half)]
    return jnp.concatenate([q[:, s:s + 640] for s in starts], 0), 64 - 64 * parity


def own_kernel(half, q, own, qpos, kpos, out, keys, here, places, sems):
    rows, kb = q.shape[0], own.shape[1]
    chunks = q.shape[1] // (half * LAT)
    parts = chunks // 2
    copies = [
        pltpu.make_async_copy(qpos, places.at[0:1, pl.ds(0, rows)], sems.at[parts]),
        pltpu.make_async_copy(kpos, places.at[1:2, :], sems.at[parts + 1]),
    ]
    for i in range(parts):
        lanes = pl.ds(i * 2 * half * LAT, 2 * half * LAT)
        copies.append(pltpu.make_async_copy(q.at[:, lanes], here.at[:, lanes], sems.at[i]))
    for copy in copies:
        copy.start()
    keys[:64, :] = jnp.zeros((64, kb), jnp.bfloat16)
    keys[64:64 + LAT, :] = own[:LAT, :]
    keys[64 + LAT:, :] = jnp.zeros((64, kb), jnp.bfloat16)
    copies[0].wait()
    copies[1].wait()
    causal = places[1:2, :].astype(jnp.float32) <= column(places[0:1, :rows], 0, rows)
    for j in range(chunks):
        if j % 2 == 0:
            copies[2 + j // 2].wait()
        lhs, first = chunk_rows(here, j, half)
        s = dot(lhs, keys[first:first + 640, :])
        for i in range(half):
            ex = jnp.exp2(s[i * rows:(i + 1) * rows] * (SCORE_SCALE * LOG2E))
            at = (j * half + i) * rows
            out[at:at + rows, :] = jnp.where(causal, ex, 0.0)


def main_kernel(half, place, q, own, a, b, c, own_exp, outside, qpos, kpos, *rest):
    outs, rest = rest[:GROUPS], rest[GROUPS:]
    e, inv, (keys, out_exp, mass) = rest[:BUFFERS], rest[BUFFERS:2 * BUFFERS], rest[2 * BUFFERS:]
    z, position = place[0], place[1]
    rows, kb = q.shape[0], own.shape[1]
    chunks = q.shape[1] // (half * LAT)
    window = STEPS * kb
    front = window - kb
    present = [jnp.where(position >= STEPS - 1 - i, 1.0, 0.0).astype(jnp.float32) for i in range(STEPS)]
    lane = lax.broadcasted_iota(jnp.int32, (32, 128), 1)

    keys[:64, :] = jnp.zeros((64, window), jnp.bfloat16)
    keys[64 + LAT:, :] = jnp.zeros((64, window), jnp.bfloat16)
    for block, slot in zip((own, a, b, c), slots_of(position)):
        keys[64:64 + LAT, pl.ds(pl.multiple_of(slot * kb, kb), kb)] = block[:LAT, :]
    out_exp[...] = jnp.exp(turned_tall(outside[...], NEGATIVE))
    mass[...] = jnp.zeros_like(mass)
    worst = [jnp.zeros((32, 1), jnp.float32)]

    def exp_unit(j, i, r):
        buffer, at = j % BUFFERS, i * rows + r
        own_rows = slice(j * half * rows + at, j * half * rows + at + 32)
        head = (j - j % 2) * half + 2 * i + j % 2
        total = jnp.where(lane == head, out_exp[r:r + 32, :], 0.0)
        for block in range(STEPS):
            piece = own_exp[own_rows, :] if block == STEPS - 1 else e[buffer][at:at + 32, block * kb:(block + 1) * kb]
            sums = piece[:, :128]
            for k in range(128, kb, 128):
                sums = sums + piece[:, k:k + 128]
            total = total + (sums if block == STEPS - 1 else sums * present[block])
        total = jnp.sum(total, axis=1, keepdims=True)
        inv[buffer][at:at + 32, :] = jnp.broadcast_to(1.0 / total, (32, 128))
        worst[0] = jnp.maximum(worst[0], total)

    def mass_unit(j, r, w):
        buffer = j % BUFFERS
        total = mass[r:r + 32, w:w + 256]
        for i in range(half):
            at = i * rows + r
            if w < front:
                piece = e[buffer][at:at + 32, w:w + 256]
            else:
                first = j * half * rows + at
                piece = own_exp[first:first + 32, w - front:w - front + 256]
            scale = inv[buffer][at:at + 32, :]
            total = total + piece * jnp.concatenate([scale, scale], 1)
        mass[r:r + 32, w:w + 256] = total

    exps = [(i, r) for i in range(half) for r in range(0, rows, 32)]
    sums = [(r, w) for r in range(0, rows, 32) for w in range(0, window, 256)]
    thirds = STEPS - 1
    for j in range(chunks + 2):
        if j < chunks:
            lhs, first = chunk_rows(q, j, half)
        for n in range(thirds):
            if j < chunks:
                lanes = slice(n * kb, (n + 1) * kb)
                s = dot(lhs, keys[first:first + 640, lanes])
                e[j % BUFFERS][:, lanes] = jnp.exp2(s * (SCORE_SCALE * LOG2E))
            if 1 <= j <= chunks:
                for i, r in exps[n * len(exps) // thirds:(n + 1) * len(exps) // thirds]:
                    exp_unit(j - 1, i, r)
            if j >= 2:
                for r, w in sums[n * len(sums) // thirds:(n + 1) * len(sums) // thirds]:
                    mass_unit(j - 2, r, w)

    @pl.when(jnp.logical_not(jnp.max(worst[0]) < SAFE))
    def _():
        slot = lax.broadcasted_iota(jnp.int32, (rows, window), 1) // kb
        causal = kpos[...].astype(jnp.float32) <= column(qpos[...], 0, rows)
        causal = jnp.concatenate([jnp.ones((rows, front), jnp.float32), jnp.where(causal, 1.0, 0.0)], 1) > 0
        visible = (position >= STEPS - 1 - slot) & causal
        line = lax.broadcasted_iota(jnp.int32, outside.shape, 0)
        mass[...] = jnp.zeros_like(mass)
        for parity in range(2):

            def exact(i, carry, parity=parity):
                first = 64 - 64 * parity
                at = pl.multiple_of(1152 * i + 512 * parity, 128)
                scores = dot(q[:, pl.ds(at, 640)], keys[first:first + 640, :]) * SCORE_SCALE
                masked = jnp.where(visible, scores, NEGATIVE)
                mine = jnp.sum(jnp.where(line == 2 * i + parity, outside[...], 0.0), axis=0, keepdims=True)
                mine = column(mine, 0, rows)
                top = jnp.maximum(jnp.max(masked, axis=1, keepdims=True), mine)
                ex = jnp.exp(masked - top)
                total = jnp.sum(ex, axis=1, keepdims=True) + jnp.exp(mine - top)
                mass[...] += ex * (1.0 / total)
                return carry

            lax.fori_loop(0, outside.shape[0] // 2, exact, 0)

    for block in range(STEPS - 1):
        lanes = slice(block * kb, (block + 1) * kb)
        mass[:, lanes] = mass[:, lanes] * present[block]
    share = rows // GROUPS
    for d in range(GROUPS):
        at = pl.ds(pl.multiple_of((z ^ d) * share, share), share)
        if d == 0:
            outs[d][...] = mass[at, :]
        else:
            coded_rows(outs[d], mass[at, :])


def heads_of(piece, count):
    return jnp.concatenate([piece[:, IDIM * j:IDIM * (j + 1)] for j in range(count)], 0)


def index_kernel(count, place, own, a, b, c, *rest):
    pieces, (score, gate, turned, keys) = rest[:GROUPS], rest[GROUPS:]
    share = score.shape[0]
    tile = count * share
    gathered(place[1], (own, a, b, c), keys, 0)
    total = jnp.zeros(score.shape, jnp.float32)
    for d in range(GROUPS):
        piece = pieces[d][...]
        scaled = weights_of(piece, IDIM * count, count) * (IDIM ** -0.5)
        rows = heads_of(piece, count)
        act = dot(rows, keys[...])
        gate[d * tile:(d + 1) * tile, :] = jnp.where(act > 0, 1.0, 0.0).astype(jnp.bfloat16)
        for j in range(count):
            total = total + jnp.maximum(act[j * share:(j + 1) * share], 0.0) * scaled[:, j:j + 1]
        tall = jnp.concatenate([jnp.broadcast_to(scaled[:, j:j + 1], (share, IDIM)) for j in range(count)], 0)
        high, low = split(rows.astype(jnp.float32) * tall)
        turned[:IDIM, d * tile:(d + 1) * tile] = high.T
        turned[IDIM:, d * tile:(d + 1) * tile] = low.T
    score[...] = total


def dscore_kernel(place, m0, m1, m2, m3, score, outside, qpos, kpos, spread, code):
    z, position = place[0], place[1]
    share, window = score.shape
    kb = kpos.shape[1]
    mass = (m0[...] + restored_rows(m1, window)) + (restored_rows(m2, window) + restored_rows(m3, window))
    target = mass / jnp.sum(mass, axis=1, keepdims=True)
    slot = lax.broadcasted_iota(jnp.int32, (share, window), 1) // kb
    causal = kpos[...].astype(jnp.float32) <= column(qpos[...], z * share, share)
    masked = jnp.where(position >= STEPS - 1 - slot, score[...], NEGATIVE)
    masked = jnp.concatenate([masked[:, :window - kb], jnp.where(causal, masked[:, window - kb:], NEGATIVE)], 1)
    out = column(outside[...], z * share, share)
    top = jnp.maximum(jnp.max(masked, axis=1, keepdims=True), out)
    expo = jnp.exp(masked - top)
    total = jnp.sum(expo, axis=1, keepdims=True) + jnp.exp(out - top)
    dscore = (expo / total - target) * float(window)
    spread[0], spread[1] = split(dscore)
    coded_rows(code, dscore)


def keys_kernel(count, gate, turned, spread, *outs):
    tile = count * spread.shape[1]
    total = None
    for d in range(GROUPS):
        rows = slice(d * tile, (d + 1) * tile)
        mask = gate[rows, :]
        both = dot(turned[:, rows], mask * jnp.concatenate([spread[0]] * count, 0))
        low = dot(turned[:IDIM, rows], mask * jnp.concatenate([spread[1]] * count, 0))
        part = both[:IDIM] + both[IDIM:] + low
        total = part if total is None else total + part
    kb = outs[STEPS - 1].shape[0]
    for i in range(STEPS):
        part = total[:, i * kb:(i + 1) * kb].T
        if i < STEPS - 1:
            coded_columns(outs[i], part)
        else:
            outs[i][...] = part


def query_kernel(heads, group, place, own, a, b, c, query, weight, c0, c1, c2, c3, *rest):
    first = heads[0]
    if first:
        (done, before), rest = rest[:2], rest[2:]
    grad, out, keys, turned, high, low, scale, tall = rest
    share, rows = c0.shape[0], query.shape[0]
    window = keys.shape[1]
    gathered(place[1], (own, a, b, c), keys, 0)
    turned[...] = keys[...].T
    for d, code in enumerate((c0, c1, c2, c3)):
        at = pl.ds(pl.multiple_of((place[0] ^ d) * share, share), share)
        high[at, :], low[at, :] = split(code[:, :window].astype(jnp.float32))
        scale[at, :] = scale_of(code[:, window:]) * (IDIM ** -0.5)
    tall[...] = turned_tall(weight[...])
    lane = lax.broadcasted_iota(jnp.int32, (rows, 128), 1)
    total = before[...] if first else jnp.zeros((rows, 128), jnp.float32)
    if first:
        grad[:, :IDIM * first] = done[:, :IDIM * first]
    for g in range(*heads, group):
        tile = heads_of(query[:, IDIM * g:IDIM * (g + group)], group)
        mask = jnp.where(dot(tile, keys[...]) > 0, 1.0, 0.0).astype(jnp.bfloat16)
        part = dot(mask * jnp.concatenate([high[...]] * group, 0), turned[...])
        part = part + dot(mask * jnp.concatenate([low[...]] * group, 0), turned[...])
        for j in range(g, g + group):
            lanes = slice(IDIM * j, IDIM * (j + 1))
            mine = part[(j - g) * rows:(j - g + 1) * rows] * scale[...]
            grad[:, lanes] = (mine * tall[:, j:j + 1]).astype(jnp.bfloat16)
            product = jnp.sum(mine * query[:, lanes].astype(jnp.float32), axis=1, keepdims=True)
            total = jnp.where(lane == j, product, total)
    out[...] = total.T[:out.shape[0], :] if first else total


def owned_kernel(p0, c1, c2, c3, after, code):
    kb = p0.shape[0]
    moved = [restored_columns(c, kb) for c in (c1, c2, c3)]
    coded_columns(code, (p0[...] + moved[0]) + (moved[1] + moved[2]))


def total_kernel(c0, c1, c2, c3, out):
    parts = [restored_columns(c, out.shape[0]) for c in (c0, c1, c2, c3)]
    out[...] = (parts[0] + parts[1]) + (parts[2] + parts[3])


SMEM = pl.BlockSpec(memory_space=pltpu.SMEM)
HBM = pl.BlockSpec(memory_space=pltpu.HBM)


def held(array):
    return pltpu.with_memory_space_constraint(array, pltpu.HBM)


def whole(array):
    rank = len(array.shape)
    return pl.BlockSpec(array.shape, lambda i: (0,) * rank)


def params(mib):
    return pltpu.CompilerParams(vmem_limit_bytes=mib << 20)


def cost(flops, size):
    return pl.CostEstimate(flops=1, bytes_accessed=1, transcendentals=0)


def along(x, axis, route):
    return lax.ppermute(x, axis, [(i, j) for i, j in route if 0 <= j < lax.axis_size(axis)])


def shards(
    main_query,
    latent,
    main_outside,
    index_query,
    index_weights,
    index_keys,
    index_outside,
    query_pos,
    key_pos,
):
    rows = main_query.shape[0]
    kb = latent.shape[0]
    heads = main_outside.shape[1]
    count = index_weights.shape[1]
    share = rows // GROUPS
    window = STEPS * kb
    n_seq = lax.axis_size("seq")
    z, position = lax.axis_index("head"), lax.axis_index("seq")
    place = jnp.stack([z, position]).astype(jnp.int32)
    bf16, f32, int16 = jnp.bfloat16, jnp.float32, jnp.int16

    def shape(dims, kind):
        return jax.ShapeDtypeStruct(dims, kind)

    def exchanged(x, d):
        return along(x, "head", [(i, i ^ d) for i in range(GROUPS)])

    weights = index_weights.T
    outsides = main_outside.T
    qpos = query_pos.reshape(1, rows)
    kpos = key_pos.reshape(1, kb)
    outside = index_outside.reshape(1, rows)
    piece_shape = (share, IDIM * count + 128)
    pack_shape = (LAT + IDIM, kb)
    packed, *mine = pl.pallas_call(
        pack_kernel,
        grid=(1,),
        in_specs=[SMEM] + [HBM] * 4,
        out_specs=[pl.BlockSpec(pack_shape, lambda i: (0, 0))]
        + [pl.BlockSpec(piece_shape, lambda i: (0, 0))] * GROUPS,
        out_shape=[shape(pack_shape, bf16)] + [shape(piece_shape, bf16)] * GROUPS,
        scratch_shapes=[
            pltpu.VMEM((rows, 128), bf16),
            pltpu.VMEM((kb, IDIM), bf16),
            pltpu.VMEM((count, rows), f32),
            pltpu.SemaphoreType.DMA((3 + GROUPS,)),
        ],
        compiler_params=params(16),
        cost_estimate=cost(0, 4 * rows * count * IDIM),
        name="pack_rows",
    )(place, *[held(x) for x in (latent.T, index_keys, index_query, weights)])
    route_b = along(packed, "seq", [(i, i + (3 if i % 2 == 0 else 1)) for i in range(n_seq)])
    route_a = along(packed, "seq", [(i, i + (1 if i % 2 == 0 else 3)) for i in range(n_seq)])
    pieces = [mine[0]] + [exchanged(mine[d], d) for d in range(1, GROUPS)]

    half = PER_STEP // 2
    own_exp = pl.pallas_call(
        functools.partial(own_kernel, half),
        grid=(1,),
        in_specs=[HBM, whole(packed), HBM, HBM],
        out_specs=pl.BlockSpec((heads * rows, kb), lambda i: (0, 0)),
        out_shape=shape((heads * rows, kb), f32),
        scratch_shapes=[
            pltpu.VMEM((704, kb), bf16),
            pltpu.VMEM(main_query.shape, bf16),
            pltpu.VMEM((8, kb), jnp.int32),
            pltpu.SemaphoreType.DMA((heads // PER_STEP + 2,)),
        ],
        compiler_params=params(24),
        cost_estimate=cost(2 * heads * rows * kb * LAT, heads * rows * (2 * LAT + 4 * kb)),
        name="own_block",
    )(held(main_query), packed, held(qpos), held(kpos))

    route_b, own_exp, pieces[1], pieces[2] = lax.optimization_barrier((route_b, own_exp, pieces[1], pieces[2]))
    route_c = along(route_b, "seq", [(i, i ^ 1) for i in range(n_seq)])
    blocks = (packed, route_a, route_b, route_c)
    code_shape = (share, window + 128)
    mass = pl.pallas_call(
        functools.partial(main_kernel, half),
        grid=(1,),
        in_specs=[SMEM] + [whole(x) for x in (main_query, *blocks, own_exp, outsides, qpos, kpos)],
        out_specs=[pl.BlockSpec((share, window), lambda i: (0, 0))]
        + [pl.BlockSpec(code_shape, lambda i: (0, 0))] * (GROUPS - 1),
        out_shape=[shape((share, window), f32)] + [shape(code_shape, int16)] * (GROUPS - 1),
        scratch_shapes=[pltpu.VMEM((half * rows, window - kb), f32)] * BUFFERS
        + [pltpu.VMEM((half * rows, 128), f32)] * BUFFERS
        + [
            pltpu.VMEM((704, window), bf16),
            pltpu.VMEM((rows, 128), f32),
            pltpu.VMEM((rows, window), f32),
        ],
        compiler_params=params(32),
        cost_estimate=cost(2 * heads * rows * window * LAT, heads * rows * 2 * LAT),
        name="main_mass",
    )(place, main_query, *blocks, own_exp, outsides, qpos, kpos)
    masses = [mass[0]] + [exchanged(mass[d], d) for d in range(1, GROUPS)]

    tile = count * share
    key_spec = pl.BlockSpec((IDIM, kb), lambda i: (0, 0))
    key_rows = [x[LAT:] for x in blocks]
    score, gate, turned = pl.pallas_call(
        functools.partial(index_kernel, count),
        grid=(1,),
        in_specs=[SMEM] + [key_spec] * 4 + [whole(x) for x in pieces],
        out_specs=[
            pl.BlockSpec((share, window), lambda i: (0, 0)),
            pl.BlockSpec((GROUPS * tile, window), lambda i: (0, 0)),
            pl.BlockSpec((2 * IDIM, GROUPS * tile), lambda i: (0, 0)),
        ],
        out_shape=[
            shape((share, window), f32),
            shape((GROUPS * tile, window), bf16),
            shape((2 * IDIM, GROUPS * tile), bf16),
        ],
        scratch_shapes=[pltpu.VMEM((IDIM, window), bf16)],
        compiler_params=params(24),
        cost_estimate=cost(4 * GROUPS * tile * window * IDIM, GROUPS * tile * window * 2),
        name="index_scores",
    )(place, *key_rows, *pieces)

    spread, code = pl.pallas_call(
        dscore_kernel,
        grid=(1,),
        in_specs=[SMEM] + [whole(x) for x in (*masses, score, outside, qpos, kpos)],
        out_specs=[
            pl.BlockSpec((2, share, window), lambda i: (0, 0, 0)),
            pl.BlockSpec(code_shape, lambda i: (0, 0)),
        ],
        out_shape=[shape((2, share, window), bf16), shape(code_shape, int16)],
        compiler_params=params(16),
        cost_estimate=cost(0, 12 * share * window),
        name="dscores",
    )(place, *masses, score, outside, qpos, kpos)
    codes = [code] + [exchanged(code, d) for d in range(1, GROUPS)]

    sum_shape = (kb + 16, IDIM)
    parts = pl.pallas_call(
        functools.partial(keys_kernel, count),
        grid=(1,),
        in_specs=[whole(gate), whole(turned), whole(spread)],
        out_specs=[pl.BlockSpec(sum_shape, lambda i: (0, 0))] * (STEPS - 1)
        + [pl.BlockSpec((kb, IDIM), lambda i: (0, 0))],
        out_shape=[shape(sum_shape, int16)] * (STEPS - 1) + [shape((kb, IDIM), f32)],
        compiler_params=params(24),
        cost_estimate=cost(8 * GROUPS * tile * window * IDIM, GROUPS * tile * window * 2),
        name="key_grads",
    )(gate, turned, spread)
    sent = [parts[STEPS - 1 - distance] for distance in range(1, STEPS)]
    sent[-1], *codes = lax.optimization_barrier((sent[-1], *codes))
    moved = [along(x, "seq", [(i, i - d - 1) for i in range(n_seq)]) for d, x in enumerate(sent)]

    group = count // 4

    def query_grads(first, last, before):
        sums_shape = (count, rows) if first else (rows, 128)
        return pl.pallas_call(
            functools.partial(query_kernel, (first, last), group),
            grid=(1,),
            in_specs=[SMEM] + [key_spec] * 4
            + [whole(x) for x in (index_query, weights, *codes)]
            + [whole(x) for x in before],
            out_specs=[
                pl.BlockSpec((rows, IDIM * count), lambda i: (0, 0)),
                pl.BlockSpec(sums_shape, lambda i: (0, 0)),
            ],
            out_shape=[shape((rows, IDIM * count), bf16), shape(sums_shape, f32)],
            scratch_shapes=[
                pltpu.VMEM((IDIM, window), bf16),
                pltpu.VMEM((window, IDIM), bf16),
                pltpu.VMEM((rows, window), bf16),
                pltpu.VMEM((rows, window), bf16),
                pltpu.VMEM((rows, 128), f32),
                pltpu.VMEM((rows, 128), f32),
            ],
            compiler_params=params(24),
            cost_estimate=cost(8 * rows * (last - first) * window * IDIM, 8 * rows * count * IDIM),
            name="query_grads",
        )(place, *key_rows, index_query, weights, *codes, *before)

    begun = query_grads(0, group, ())
    grad_query, grad_weight = query_grads(group, count, begun)

    owned = pl.pallas_call(
        owned_kernel,
        grid=(1,),
        in_specs=[whole(x) for x in (parts[STEPS - 1], *moved, begun[1])],
        out_specs=pl.BlockSpec(sum_shape, lambda i: (0, 0)),
        out_shape=shape(sum_shape, int16),
        compiler_params=params(16),
        cost_estimate=cost(0, 20 * kb * IDIM),
        name="owned_keys",
    )(parts[STEPS - 1], *moved, begun[1])
    owners = [owned] + [exchanged(owned, d) for d in range(1, GROUPS)]
    grad_keys = pl.pallas_call(
        total_kernel,
        grid=(1,),
        in_specs=[whole(x) for x in owners],
        out_specs=pl.BlockSpec((kb, IDIM), lambda i: (0, 0)),
        out_shape=shape((kb, IDIM), f32),
        compiler_params=params(16),
        cost_estimate=cost(0, 12 * kb * IDIM),
        name="total_keys",
    )(*owners)
    return (grad_query, grad_weight.T, grad_keys)


def any_shards(main_query, latent, main_outside, index_query, index_weights, index_keys, *rest):
    args = (main_query, latent, main_outside, index_query, index_weights, index_keys, *rest)
    fits = (
        lax.axis_size("head") == GROUPS
        and lax.axis_size("seq") % 2 == 0
        and main_query.shape[0] == 128
        and main_outside.shape[1] % PER_STEP == 0
        and main_outside.shape[1] <= 128
        and latent.shape[0] % 256 == 0
        and latent.shape[1] == LAT
        and 3 * index_weights.shape[1] <= 128
        and index_weights.shape[1] % 16 == 0
    )
    return shards(*args) if fits else plain_shards(*args)


def solution(mesh):
    in_specs = (
        P("seq", "head"),
        P("seq", None),
        P("seq", "head"),
        P("seq", "head"),
        P("seq", "head"),
        P("seq", None),
        P("seq"),
        P("seq"),
        P("seq"),
    )
    out_specs = (P("seq", "head"), P("seq", "head"), P("seq", None))
    return jax.shard_map(any_shards, mesh=mesh, in_specs=in_specs, out_specs=out_specs, check_vma=False)
```

```python
import functools

import jax
import jax.numpy as jnp
from jax import lax
from jax.experimental import pallas as pl
from jax.experimental.pallas import tpu as pltpu
from jax.sharding import PartitionSpec as P

IDIM = 128
KB = 256
STEPS = 4


NEGATIVE = -1e30
SCORE_SCALE = 192.0 ** (-0.5)


def passed_along(block, axis, distance):
    devices = range(lax.axis_size(axis))
    route = [(i - distance, i) for i in devices if i - distance in devices]
    return lax.ppermute(block, axis, route)


def head_mass(scores, visible, outside):
    masked = jnp.where(visible[None], scores, NEGATIVE)
    highest = jnp.maximum(jnp.max(masked, axis=2), outside.T)
    expo = jnp.exp(masked - highest[:, :, None])
    total = jnp.sum(expo, axis=2) + jnp.exp(outside.T - highest)
    return jnp.sum(expo / total[:, :, None], axis=0)


def score_grad(mass, index_score, visible, outside):
    target = mass / jnp.sum(mass, axis=1, keepdims=True)
    masked = jnp.where(visible, index_score, NEGATIVE)
    highest = jnp.maximum(jnp.max(masked, axis=1), outside)
    expo = jnp.exp(masked - highest[:, None])
    total = jnp.sum(expo, axis=1) + jnp.exp(outside - highest)
    return (expo / total[:, None] - target) * (STEPS * KB)


def plain_shards(
    main_query,
    latent,
    main_outside,
    index_query,
    index_weights,
    index_keys,
    index_outside,
    query_pos,
    key_pos,
):
    query_rows = main_query.shape[0]
    block_keys = latent.shape[0]
    width = latent.shape[1]
    local_heads = main_outside.shape[1]
    local_index = index_weights.shape[1]
    index_width = index_keys.shape[1]
    window = STEPS * block_keys
    factor = IDIM ** (-0.5)
    position = lax.axis_index("seq")
    latent_parts = []
    index_parts = []
    for distance in range(STEPS - 1, 0, -1):
        latent_parts.append(passed_along(latent, "seq", distance))
        index_parts.append(passed_along(index_keys, "seq", distance))
    latent_window = jnp.concatenate(latent_parts + [latent], 0)
    key_window = jnp.concatenate(index_parts + [index_keys], 0)
    slot_block = jnp.arange(window, dtype=jnp.int32) // block_keys
    lagging = STEPS - 1 - slot_block
    places_full = jnp.concatenate([jnp.zeros((window - block_keys,), jnp.int32), key_pos], 0)
    causal = (slot_block < STEPS - 1)[None, :] | (places_full[None, :] <= query_pos[:, None])
    visible = (position >= lagging)[None, :] & causal
    queries = main_query.reshape(query_rows, local_heads, width)
    scores = (
        jnp.einsum("qhc,wc->hqw", queries, latent_window, preferred_element_type=jnp.float32)
        * SCORE_SCALE
    )
    mass_part = head_mass(scores, visible, main_outside)
    index_rows = index_query.reshape(query_rows, local_index, index_width)
    activity = (
        jnp.einsum("qjd,wd->jqw", index_rows, key_window, preferred_element_type=jnp.float32)
        * factor
    )
    rectified = jnp.maximum(activity, 0.0)
    index_part = jnp.einsum("qj,jqw->qw", index_weights, rectified)
    mass, index_score = (
        lax.psum_scatter(mass_part, "head", scatter_dimension=0, tiled=True),
        lax.psum_scatter(index_part, "head", scatter_dimension=0, tiled=True),
    )
    share = mass.shape[0]
    start = lax.axis_index("head") * share
    visible_rows = lax.dynamic_slice_in_dim(visible, start, share, 0)
    outside_rows = lax.dynamic_slice_in_dim(index_outside, start, share, 0)
    dscore = lax.all_gather(
        score_grad(mass, index_score, visible_rows, outside_rows), "head", axis=0, tiled=True
    )
    gated = dscore[None] * index_weights.T[:, :, None] * (activity > 0).astype(jnp.float32)
    key_wide = key_window.astype(jnp.float32)
    rows_wide = index_rows.astype(jnp.float32)
    grad_query = (
        jnp.einsum("jqw,wd->qjd", gated, key_wide, precision=lax.Precision.HIGHEST) * factor
    )
    grad_query = grad_query.astype(jnp.bfloat16).reshape(query_rows, local_index * index_width)
    grad_weight = jnp.einsum("qw,jqw->qj", dscore, rectified)
    grad_window = (
        jnp.einsum("jqw,qjd->wd", gated, rows_wide, precision=lax.Precision.HIGHEST) * factor
    )
    grad_parts = grad_window.reshape(STEPS, block_keys, index_width)
    grad_total = grad_parts[STEPS - 1]
    for distance in range(1, STEPS):
        grad_total = grad_total + passed_along(grad_parts[STEPS - 1 - distance], "seq", -distance)
    grad_keys = lax.psum(grad_total, "head")
    return (grad_query, grad_weight, grad_keys)


LOG2E = 1.4426950408889634
LAT = 576
GROUPS = 4
BUFFERS = 4
PER_STEP = 8
SAFE = 1e30
LEVELS = 32000.0
NN = (((1,), (0,)), ((), ()))
NT = (((1,), (1,)), ((), ()))


def dot(a, b, dims=NN):
    return lax.dot_general(a, b, dims, preferred_element_type=jnp.float32)


def split(x):
    high = x.astype(jnp.bfloat16)
    return high, (x - high.astype(jnp.float32)).astype(jnp.bfloat16)


def coded(x, axis):
    top = jnp.max(jnp.abs(x), axis=axis, keepdims=True)
    power = jnp.ceil(8.0 * jnp.log2(jnp.maximum(top, 1e-30)))
    code = jnp.floor(x * (LEVELS * jnp.exp2(power * -0.125)) + 0.5)
    return code.astype(jnp.int32).astype(jnp.int16), power.astype(jnp.int32).astype(jnp.int16)


def scale_of(power):
    return jnp.exp2(power.astype(jnp.float32) * 0.125) * (1.0 / LEVELS)


def coded_rows(ref, x):
    code, power = coded(x, 1)
    ref[:, :x.shape[1]] = code
    ref[:, x.shape[1]:] = jnp.broadcast_to(power.astype(jnp.int32), (x.shape[0], 128)).astype(jnp.int16)


def restored_rows(ref, window):
    return ref[:, :window].astype(jnp.float32) * scale_of(ref[:, window:])[:, :1]


def coded_columns(ref, x):
    code, power = coded(x, 0)
    ref[:x.shape[0], :] = code
    ref[x.shape[0]:, :] = jnp.broadcast_to(power.astype(jnp.int32), (16, x.shape[1])).astype(jnp.int16)


def restored_columns(ref, count):
    return ref[:count, :].astype(jnp.float32) * scale_of(ref[count:, :])[:1, :]


def column(row, first, count):
    lane = lax.broadcasted_iota(jnp.int32, (count, 128), 1)
    line = lax.broadcasted_iota(jnp.int32, (count, 128), 0) + first
    wide = jnp.broadcast_to(row.astype(jnp.float32), (count, 128))
    return jnp.sum(jnp.where(lane == line, wide, 0.0), axis=1, keepdims=True)


def turned_tall(x, value=0.0):
    fill = jnp.full((128 - x.shape[0], 128), value, jnp.float32)
    return jnp.concatenate([x, fill], 0).T


def slots_of(position):
    even = lax.rem(position, 2) == 0
    return 3, jnp.where(even, 0, 2), jnp.where(even, 2, 0), 1


def gathered(position, blocks, kept, first):
    kb = blocks[0].shape[1]
    for block, slot in zip(blocks, slots_of(position)):
        at = pl.ds(pl.multiple_of(slot * kb, kb), kb)
        kept[first:first + block.shape[0], at] = block[...]


def heads_at(q, parity):
    starts = [1152 * i + 512 * parity for i in range(q.shape[1] // 1152)]
    return jnp.concatenate([q[:, s:s + 640] for s in starts], 0)


def pack_kernel(place, latent, keys, query, weight, packed, *rest):
    outs, (kept, keys_here, weight_here, sems) = rest[:GROUPS], rest[GROUPS:]
    share = outs[0].shape[0]
    width, count = query.shape[1], weight.shape[0]
    copies = [
        pltpu.make_async_copy(latent, packed.at[pl.ds(0, LAT), :], sems.at[0]),
        pltpu.make_async_copy(keys, keys_here, sems.at[1]),
        pltpu.make_async_copy(weight, weight_here, sems.at[2]),
    ]
    for d in range(GROUPS):
        at = pl.ds(pl.multiple_of((place[0] ^ d) * share, share), share)
        here = outs[d].at[:, pl.ds(0, width)]
        copies.append(pltpu.make_async_copy(query.at[at, :], here, sems.at[3 + d]))
    for copy in copies:
        copy.start()
    copies[1].wait()
    packed[LAT:, :] = keys_here[...].T
    copies[2].wait()
    tall = turned_tall(weight_here[...])[:, :count]
    high = tall.astype(jnp.bfloat16)
    middle, low = split(tall - high.astype(jnp.float32))
    kept[...] = jnp.concatenate([high, middle, low, jnp.zeros((128, 128 - 3 * count), jnp.bfloat16)], 1)
    for d in range(GROUPS):
        at = pl.ds(pl.multiple_of((place[0] ^ d) * share, share), share)
        outs[d][:, width:] = kept[at, :]
    copies[0].wait()
    for copy in copies[3:]:
        copy.wait()


def weights_of(piece, width, count):
    tail = piece[:, width:].astype(jnp.float32)
    return tail[:, :count] + tail[:, count:2 * count] + tail[:, 2 * count:3 * count]


def chunk_rows(q, j, half):
    parity, pair = j % 2, half * (j // 2)
    starts = [1152 * (pair + i) + 512 * parity for i in range(half)]
    return jnp.concatenate([q[:, s:s + 640] for s in starts], 0), 64 - 64 * parity


def own_kernel(half, q, own, qpos, kpos, out, keys, here, places, sems):
    rows, kb = q.shape[0], own.shape[1]
    chunks = q.shape[1] // (half * LAT)
    parts = chunks // 2
    copies = [
        pltpu.make_async_copy(qpos, places.at[0:1, pl.ds(0, rows)], sems.at[parts]),
        pltpu.make_async_copy(kpos, places.at[1:2, :], sems.at[parts + 1]),
    ]
    for i in range(parts):
        lanes = pl.ds(i * 2 * half * LAT, 2 * half * LAT)
        copies.append(pltpu.make_async_copy(q.at[:, lanes], here.at[:, lanes], sems.at[i]))
    for copy in copies:
        copy.start()
    keys[:64, :] = jnp.zeros((64, kb), jnp.bfloat16)
    keys[64:64 + LAT, :] = own[:LAT, :]
    keys[64 + LAT:, :] = jnp.zeros((64, kb), jnp.bfloat16)
    copies[0].wait()
    copies[1].wait()
    causal = places[1:2, :].astype(jnp.float32) <= column(places[0:1, :rows], 0, rows)
    for j in range(chunks):
        if j % 2 == 0:
            copies[2 + j // 2].wait()
        lhs, first = chunk_rows(here, j, half)
        s = dot(lhs, keys[first:first + 640, :])
        for i in range(half):
            ex = jnp.exp2(s[i * rows:(i + 1) * rows] * (SCORE_SCALE * LOG2E))
            at = (j * half + i) * rows
            out[at:at + rows, :] = jnp.where(causal, ex, 0.0)


def block_kernel(half, q, block, out, keys):
    rows, kb = q.shape[0], block.shape[1]
    keys[:64, :] = jnp.zeros((64, kb), jnp.bfloat16)
    keys[64:64 + LAT, :] = block[:LAT, :]
    keys[64 + LAT:, :] = jnp.zeros((64, kb), jnp.bfloat16)
    size = half * rows
    for j in range(q.shape[1] // (half * LAT)):
        lhs, first = chunk_rows(q, j, half)
        out[j * size:(j + 1) * size, :] = jnp.exp2(dot(lhs, keys[first:first + 640, :]) * (SCORE_SCALE * LOG2E))


def main_kernel(half, place, q, own, a, b, c, own_exp, b_exp, outside, qpos, kpos, *rest):
    outs, rest = rest[:GROUPS], rest[GROUPS:]
    e, inv, (keys, out_exp, mass) = rest[:BUFFERS], rest[BUFFERS:2 * BUFFERS], rest[2 * BUFFERS:]
    z, position = place[0], place[1]
    rows, kb = q.shape[0], own.shape[1]
    chunks = q.shape[1] // (half * LAT)
    window = STEPS * kb
    own_slot, a_slot, b_slot, c_slot = slots_of(position)
    slots = (a_slot, c_slot, b_slot, own_slot)
    present = [position >= STEPS - 1 - slot for slot in slots]
    later = 2
    done = {later: b_exp, later + 1: own_exp}
    lane = lax.broadcasted_iota(jnp.int32, (32, 128), 1)

    keys[:64, :] = jnp.zeros((64, window), jnp.bfloat16)
    keys[64 + LAT:, :] = jnp.zeros((64, window), jnp.bfloat16)
    for i, block in enumerate((a, c, b, own)):
        keys[64:64 + LAT, i * kb:(i + 1) * kb] = block[:LAT, :]
    out_exp[...] = jnp.exp(turned_tall(outside[...], NEGATIVE))
    mass[...] = jnp.zeros_like(mass)
    worst = [jnp.zeros((32, 1), jnp.float32)]

    def exp_unit(j, i, r):
        buffer, at = j % BUFFERS, i * rows + r
        done_rows = slice(j * half * rows + at, j * half * rows + at + 32)
        head = (j - j % 2) * half + 2 * i + j % 2
        total = jnp.where(lane == head, out_exp[r:r + 32, :], 0.0)
        for block in range(STEPS):
            if block in done:
                piece = done[block][done_rows, :]
            else:
                piece = e[buffer][at:at + 32, block * kb:(block + 1) * kb]
            sums = piece[:, :128]
            for k in range(128, kb, 128):
                sums = sums + piece[:, k:k + 128]
            total = total + (sums if block == STEPS - 1 else jnp.where(present[block], sums, 0.0))
        total = jnp.sum(total, axis=1, keepdims=True)
        inv[buffer][at:at + 32, :] = jnp.broadcast_to(1.0 / total, (32, 128))
        worst[0] = jnp.maximum(worst[0], total)

    def mass_unit(j, r, w):
        buffer = j % BUFFERS
        total = mass[r:r + 32, w:w + 256]
        for i in range(half):
            at = i * rows + r
            if w // kb in done:
                first = j * half * rows + at
                piece = done[w // kb][first:first + 32, w % kb:w % kb + 256]
            else:
                piece = e[buffer][at:at + 32, w:w + 256]
            scale = inv[buffer][at:at + 32, :]
            total = total + piece * jnp.concatenate([scale, scale], 1)
        mass[r:r + 32, w:w + 256] = total

    exps = [(i, r) for i in range(half) for r in range(0, rows, 32)]
    sums = [(r, w) for r in range(0, rows, 32) for w in range(0, window, 256)]
    thirds = later
    for j in range(chunks + 2):
        if j < chunks:
            lhs, first = chunk_rows(q, j, half)
        for n in range(thirds):
            if j < chunks:
                lanes = slice(n * kb, (n + 1) * kb)
                s = dot(lhs, keys[first:first + 640, lanes])
                e[j % BUFFERS][:, lanes] = jnp.exp2(s * (SCORE_SCALE * LOG2E))
            if 1 <= j <= chunks:
                for i, r in exps[n * len(exps) // thirds:(n + 1) * len(exps) // thirds]:
                    exp_unit(j - 1, i, r)
            if j >= 2:
                for r, w in sums[n * len(sums) // thirds:(n + 1) * len(sums) // thirds]:
                    mass_unit(j - 2, r, w)

    @pl.when(jnp.logical_not(jnp.max(worst[0]) < SAFE))
    def _():
        causal = kpos[...].astype(jnp.float32) <= column(qpos[...], 0, rows)
        seen = [jnp.where(p, jnp.ones((rows, kb), jnp.float32), 0.0) for p in present[:STEPS - 1]]
        visible = jnp.concatenate(seen + [jnp.where(causal, 1.0, 0.0)], 1) > 0
        line = lax.broadcasted_iota(jnp.int32, outside.shape, 0)
        mass[...] = jnp.zeros_like(mass)
        for parity in range(2):

            def exact(i, carry, parity=parity):
                first = 64 - 64 * parity
                at = pl.multiple_of(1152 * i + 512 * parity, 128)
                scores = dot(q[:, pl.ds(at, 640)], keys[first:first + 640, :]) * SCORE_SCALE
                masked = jnp.where(visible, scores, NEGATIVE)
                mine = jnp.sum(jnp.where(line == 2 * i + parity, outside[...], 0.0), axis=0, keepdims=True)
                mine = column(mine, 0, rows)
                top = jnp.maximum(jnp.max(masked, axis=1, keepdims=True), mine)
                ex = jnp.exp(masked - top)
                total = jnp.sum(ex, axis=1, keepdims=True) + jnp.exp(mine - top)
                mass[...] += ex * (1.0 / total)
                return carry

            lax.fori_loop(0, outside.shape[0] // 2, exact, 0)

    ordered = [mass[:, i * kb:(i + 1) * kb] for i in range(STEPS)]
    ordered = [x if i == STEPS - 1 else jnp.where(present[i], x, 0.0) for i, x in enumerate(ordered)]
    for slot, x in zip(slots, ordered):
        mass[:, pl.ds(pl.multiple_of(slot * kb, kb), kb)] = x
    share = rows // GROUPS
    for d in range(GROUPS):
        at = pl.ds(pl.multiple_of((z ^ d) * share, share), share)
        if d == 0:
            outs[d][...] = mass[at, :]
        else:
            coded_rows(outs[d], mass[at, :])


def heads_of(piece, count):
    return jnp.concatenate([piece[:, IDIM * j:IDIM * (j + 1)] for j in range(count)], 0)


def index_kernel(count, place, own, a, b, c, *rest):
    pieces, (score, gate, turned, keys) = rest[:GROUPS], rest[GROUPS:]
    share = score.shape[0]
    tile = count * share
    gathered(place[1], (own, a, b, c), keys, 0)
    total = jnp.zeros(score.shape, jnp.float32)
    for d in range(GROUPS):
        piece = pieces[d][...]
        scaled = weights_of(piece, IDIM * count, count) * (IDIM ** -0.5)
        rows = heads_of(piece, count)
        act = dot(rows, keys[...])
        gate[d * tile:(d + 1) * tile, :] = jnp.where(act > 0, 1.0, 0.0).astype(jnp.bfloat16)
        for j in range(count):
            total = total + jnp.maximum(act[j * share:(j + 1) * share], 0.0) * scaled[:, j:j + 1]
        tall = jnp.concatenate([jnp.broadcast_to(scaled[:, j:j + 1], (share, IDIM)) for j in range(count)], 0)
        high, low = split(rows.astype(jnp.float32) * tall)
        turned[:IDIM, d * tile:(d + 1) * tile] = high.T
        turned[IDIM:, d * tile:(d + 1) * tile] = low.T
    score[...] = total


def dscore_kernel(place, m0, m3, m2, m1, score, outside, qpos, kpos, spread, code):
    z, position = place[0], place[1]
    share, window = score.shape
    kb = kpos.shape[1]
    mass = (m0[...] + restored_rows(m1, window)) + (restored_rows(m2, window) + restored_rows(m3, window))
    target = mass / jnp.sum(mass, axis=1, keepdims=True)
    slot = lax.broadcasted_iota(jnp.int32, (share, window), 1) // kb
    causal = kpos[...].astype(jnp.float32) <= column(qpos[...], z * share, share)
    masked = jnp.where(position >= STEPS - 1 - slot, score[...], NEGATIVE)
    masked = jnp.concatenate([masked[:, :window - kb], jnp.where(causal, masked[:, window - kb:], NEGATIVE)], 1)
    out = column(outside[...], z * share, share)
    top = jnp.maximum(jnp.max(masked, axis=1, keepdims=True), out)
    expo = jnp.exp(masked - top)
    total = jnp.sum(expo, axis=1, keepdims=True) + jnp.exp(out - top)
    dscore = (expo / total - target) * float(window)
    spread[0], spread[1] = split(dscore)
    coded_rows(code, dscore)


def keys_kernel(count, gate, turned, spread, *outs):
    tile = count * spread.shape[1]
    total = None
    for d in range(GROUPS):
        rows = slice(d * tile, (d + 1) * tile)
        mask = gate[rows, :]
        both = dot(turned[:, rows], mask * jnp.concatenate([spread[0]] * count, 0))
        low = dot(turned[:IDIM, rows], mask * jnp.concatenate([spread[1]] * count, 0))
        part = both[:IDIM] + both[IDIM:] + low
        total = part if total is None else total + part
    kb = outs[STEPS - 1].shape[0]
    for i in range(STEPS):
        part = total[:, i * kb:(i + 1) * kb].T
        if i < STEPS - 1:
            coded_columns(outs[i], part)
        else:
            outs[i][...] = part


def query_kernel(heads, group, place, own, a, b, c, query, weight, c0, c1, c2, c3, *rest):
    first = heads[0]
    if first:
        (done, before), rest = rest[:2], rest[2:]
    grad, out, keys, turned, high, low, scale, tall = rest
    share, rows = c0.shape[0], query.shape[0]
    window = keys.shape[1]
    gathered(place[1], (own, a, b, c), keys, 0)
    turned[...] = keys[...].T
    for d, code in enumerate((c0, c1, c2, c3)):
        at = pl.ds(pl.multiple_of((place[0] ^ d) * share, share), share)
        high[at, :], low[at, :] = split(code[:, :window].astype(jnp.float32))
        scale[at, :] = scale_of(code[:, window:]) * (IDIM ** -0.5)
    tall[...] = turned_tall(weight[...])
    lane = lax.broadcasted_iota(jnp.int32, (rows, 128), 1)
    total = before[...] if first else jnp.zeros((rows, 128), jnp.float32)
    if first:
        grad[:, :IDIM * first] = done[:, :IDIM * first]
    for g in range(*heads, group):
        tile = heads_of(query[:, IDIM * g:IDIM * (g + group)], group)
        mask = jnp.where(dot(tile, keys[...]) > 0, 1.0, 0.0).astype(jnp.bfloat16)
        part = dot(mask * jnp.concatenate([high[...]] * group, 0), turned[...])
        part = part + dot(mask * jnp.concatenate([low[...]] * group, 0), turned[...])
        for j in range(g, g + group):
            lanes = slice(IDIM * j, IDIM * (j + 1))
            mine = part[(j - g) * rows:(j - g + 1) * rows] * scale[...]
            grad[:, lanes] = (mine * tall[:, j:j + 1]).astype(jnp.bfloat16)
            product = jnp.sum(mine * query[:, lanes].astype(jnp.float32), axis=1, keepdims=True)
            total = jnp.where(lane == j, product, total)
    out[...] = total.T[:out.shape[0], :] if first else total


def owned_kernel(p0, c1, c2, c3, after, code):
    kb = p0.shape[0]
    moved = [restored_columns(c, kb) for c in (c1, c2, c3)]
    coded_columns(code, (p0[...] + moved[0]) + (moved[1] + moved[2]))


def total_kernel(c0, c1, c2, c3, out):
    parts = [restored_columns(c, out.shape[0]) for c in (c0, c1, c2, c3)]
    out[...] = (parts[0] + parts[1]) + (parts[2] + parts[3])


SMEM = pl.BlockSpec(memory_space=pltpu.SMEM)
HBM = pl.BlockSpec(memory_space=pltpu.HBM)


def held(array):
    return pltpu.with_memory_space_constraint(array, pltpu.HBM)


def whole(array):
    rank = len(array.shape)
    return pl.BlockSpec(array.shape, lambda i: (0,) * rank)


def params(mib):
    return pltpu.CompilerParams(vmem_limit_bytes=mib << 20)


def cost(flops, size):
    return pl.CostEstimate(flops=1, bytes_accessed=1, transcendentals=0)


def along(x, axis, route):
    size = lax.axis_size(axis)
    return lax.ppermute(x, axis, [(i, j % size) for i, j in route])


def shards(
    main_query,
    latent,
    main_outside,
    index_query,
    index_weights,
    index_keys,
    index_outside,
    query_pos,
    key_pos,
):
    rows = main_query.shape[0]
    kb = latent.shape[0]
    heads = main_outside.shape[1]
    count = index_weights.shape[1]
    share = rows // GROUPS
    window = STEPS * kb
    n_seq = lax.axis_size("seq")
    z, position = lax.axis_index("head"), lax.axis_index("seq")
    place = jnp.stack([z, position]).astype(jnp.int32)
    bf16, f32, int16 = jnp.bfloat16, jnp.float32, jnp.int16

    def shape(dims, kind):
        return jax.ShapeDtypeStruct(dims, kind)

    def exchanged(x, d):
        return along(x, "head", [(i, i ^ d) for i in range(GROUPS)])

    weights = index_weights.T
    outsides = main_outside.T
    qpos = query_pos.reshape(1, rows)
    kpos = key_pos.reshape(1, kb)
    outside = index_outside.reshape(1, rows)
    piece_shape = (share, IDIM * count + 128)
    pack_shape = (LAT + IDIM, kb)
    packed, *mine = pl.pallas_call(
        pack_kernel,
        grid=(1,),
        in_specs=[SMEM] + [HBM] * 4,
        out_specs=[pl.BlockSpec(pack_shape, lambda i: (0, 0))]
        + [pl.BlockSpec(piece_shape, lambda i: (0, 0))] * GROUPS,
        out_shape=[shape(pack_shape, bf16)] + [shape(piece_shape, bf16)] * GROUPS,
        scratch_shapes=[
            pltpu.VMEM((rows, 128), bf16),
            pltpu.VMEM((kb, IDIM), bf16),
            pltpu.VMEM((count, rows), f32),
            pltpu.SemaphoreType.DMA((3 + GROUPS,)),
        ],
        compiler_params=params(16),
        cost_estimate=cost(0, 4 * rows * count * IDIM),
        name="pack_rows",
    )(place, *[held(x) for x in (latent.T, index_keys, index_query, weights)])
    route_b = along(packed, "seq", [(i, i + (3 if i % 2 == 0 else 1)) for i in range(n_seq)])
    route_a = along(packed, "seq", [(i, i + (1 if i % 2 == 0 else 3)) for i in range(n_seq)])
    pieces = [mine[0]] + [exchanged(mine[d], d) for d in range(1, GROUPS)]

    half = PER_STEP // 2
    own_exp = pl.pallas_call(
        functools.partial(own_kernel, half),
        grid=(1,),
        in_specs=[HBM, whole(packed), HBM, HBM],
        out_specs=pl.BlockSpec((heads * rows, kb), lambda i: (0, 0)),
        out_shape=shape((heads * rows, kb), f32),
        scratch_shapes=[
            pltpu.VMEM((704, kb), bf16),
            pltpu.VMEM(main_query.shape, bf16),
            pltpu.VMEM((8, kb), jnp.int32),
            pltpu.SemaphoreType.DMA((heads // PER_STEP + 2,)),
        ],
        compiler_params=params(24),
        cost_estimate=cost(2 * heads * rows * kb * LAT, heads * rows * (2 * LAT + 4 * kb)),
        name="own_block",
    )(held(main_query), packed, held(qpos), held(kpos))

    route_b, own_exp, pieces[1], pieces[2] = lax.optimization_barrier((route_b, own_exp, pieces[1], pieces[2]))
    b_exp = pl.pallas_call(
        functools.partial(block_kernel, half),
        grid=(1,),
        in_specs=[whole(main_query), whole(route_b)],
        out_specs=pl.BlockSpec((heads * rows, kb), lambda i: (0, 0)),
        out_shape=shape((heads * rows, kb), f32),
        scratch_shapes=[pltpu.VMEM((704, kb), bf16)],
        compiler_params=params(16),
        cost_estimate=cost(2 * heads * rows * kb * LAT, heads * rows * (2 * LAT + 4 * kb)),
        name="next_block",
    )(main_query, route_b)
    route_c = along(route_b, "seq", [(i, i ^ 1) for i in range(n_seq)])
    blocks = (packed, route_a, route_b, route_c)
    code_shape = (share, window + 128)
    mass = pl.pallas_call(
        functools.partial(main_kernel, half),
        grid=(1,),
        in_specs=[SMEM] + [whole(x) for x in (main_query, *blocks, own_exp, b_exp, outsides, qpos, kpos)],
        out_specs=[pl.BlockSpec((share, window), lambda i: (0, 0))]
        + [pl.BlockSpec(code_shape, lambda i: (0, 0))] * (GROUPS - 1),
        out_shape=[shape((share, window), f32)] + [shape(code_shape, int16)] * (GROUPS - 1),
        scratch_shapes=[pltpu.VMEM((half * rows, 2 * kb), f32)] * BUFFERS
        + [pltpu.VMEM((half * rows, 128), f32)] * BUFFERS
        + [
            pltpu.VMEM((704, window), bf16),
            pltpu.VMEM((rows, 128), f32),
            pltpu.VMEM((rows, window), f32),
        ],
        compiler_params=params(32),
        cost_estimate=cost(2 * heads * rows * window * LAT, heads * rows * 2 * LAT),
        name="main_mass",
    )(place, main_query, *blocks, own_exp, b_exp, outsides, qpos, kpos)
    masses = [mass[0]] + [exchanged(mass[d], d) for d in range(1, GROUPS)]

    tile = count * share
    key_spec = pl.BlockSpec((IDIM, kb), lambda i: (0, 0))
    key_rows = [x[LAT:] for x in blocks]
    score, gate, turned = pl.pallas_call(
        functools.partial(index_kernel, count),
        grid=(1,),
        in_specs=[SMEM] + [key_spec] * 4 + [whole(x) for x in pieces],
        out_specs=[
            pl.BlockSpec((share, window), lambda i: (0, 0)),
            pl.BlockSpec((GROUPS * tile, window), lambda i: (0, 0)),
            pl.BlockSpec((2 * IDIM, GROUPS * tile), lambda i: (0, 0)),
        ],
        out_shape=[
            shape((share, window), f32),
            shape((GROUPS * tile, window), bf16),
            shape((2 * IDIM, GROUPS * tile), bf16),
        ],
        scratch_shapes=[pltpu.VMEM((IDIM, window), bf16)],
        compiler_params=params(24),
        cost_estimate=cost(4 * GROUPS * tile * window * IDIM, GROUPS * tile * window * 2),
        name="index_scores",
    )(place, *key_rows, *pieces)

    spread, code = pl.pallas_call(
        dscore_kernel,
        grid=(1,),
        in_specs=[SMEM] + [whole(x) for x in (masses[0], *masses[:0:-1], score, outside, qpos, kpos)],
        out_specs=[
            pl.BlockSpec((2, share, window), lambda i: (0, 0, 0)),
            pl.BlockSpec(code_shape, lambda i: (0, 0)),
        ],
        out_shape=[shape((2, share, window), bf16), shape(code_shape, int16)],
        compiler_params=params(16),
        cost_estimate=cost(0, 12 * share * window),
        name="dscores",
    )(place, masses[0], *masses[:0:-1], score, outside, qpos, kpos)
    codes = [code] + [exchanged(code, d) for d in range(1, GROUPS)]

    sum_shape = (kb + 16, IDIM)
    parts = pl.pallas_call(
        functools.partial(keys_kernel, count),
        grid=(1,),
        in_specs=[whole(gate), whole(turned), whole(spread)],
        out_specs=[pl.BlockSpec(sum_shape, lambda i: (0, 0))] * (STEPS - 1)
        + [pl.BlockSpec((kb, IDIM), lambda i: (0, 0))],
        out_shape=[shape(sum_shape, int16)] * (STEPS - 1) + [shape((kb, IDIM), f32)],
        compiler_params=params(24),
        cost_estimate=cost(8 * GROUPS * tile * window * IDIM, GROUPS * tile * window * 2),
        name="key_grads",
    )(gate, turned, spread)
    sent = [parts[STEPS - 1 - distance] for distance in range(1, STEPS)]
    sent[-1], codes[2] = lax.optimization_barrier((sent[-1], codes[2]))
    moved = [along(x, "seq", [(i, i - d - 1) for i in range(n_seq)]) for d, x in enumerate(sent)]

    group = count // 4

    def query_grads(first, last, before):
        sums_shape = (count, rows) if first else (rows, 128)
        return pl.pallas_call(
            functools.partial(query_kernel, (first, last), group),
            grid=(1,),
            in_specs=[SMEM] + [key_spec] * 4
            + [whole(x) for x in (index_query, weights, *codes)]
            + [whole(x) for x in before],
            out_specs=[
                pl.BlockSpec((rows, IDIM * count), lambda i: (0, 0)),
                pl.BlockSpec(sums_shape, lambda i: (0, 0)),
            ],
            out_shape=[shape((rows, IDIM * count), bf16), shape(sums_shape, f32)],
            scratch_shapes=[
                pltpu.VMEM((IDIM, window), bf16),
                pltpu.VMEM((window, IDIM), bf16),
                pltpu.VMEM((rows, window), bf16),
                pltpu.VMEM((rows, window), bf16),
                pltpu.VMEM((rows, 128), f32),
                pltpu.VMEM((rows, 128), f32),
            ],
            compiler_params=params(24),
            cost_estimate=cost(8 * rows * (last - first) * window * IDIM, 8 * rows * count * IDIM),
            name="query_grads",
        )(place, *key_rows, index_query, weights, *codes, *before)

    begun = query_grads(0, group, ())
    grad_query, grad_weight = query_grads(group, count, begun)

    owned = pl.pallas_call(
        owned_kernel,
        grid=(1,),
        in_specs=[whole(x) for x in (parts[STEPS - 1], *moved, begun[1])],
        out_specs=pl.BlockSpec(sum_shape, lambda i: (0, 0)),
        out_shape=shape(sum_shape, int16),
        compiler_params=params(16),
        cost_estimate=cost(0, 20 * kb * IDIM),
        name="owned_keys",
    )(parts[STEPS - 1], *moved, begun[1])
    owners = [owned] + [exchanged(owned, d) for d in range(1, GROUPS)]
    grad_keys = pl.pallas_call(
        total_kernel,
        grid=(1,),
        in_specs=[whole(x) for x in owners],
        out_specs=pl.BlockSpec((kb, IDIM), lambda i: (0, 0)),
        out_shape=shape((kb, IDIM), f32),
        compiler_params=params(16),
        cost_estimate=cost(0, 12 * kb * IDIM),
        name="total_keys",
    )(*owners)
    return (grad_query, grad_weight.T, grad_keys)


def any_shards(main_query, latent, main_outside, index_query, index_weights, index_keys, *rest):
    args = (main_query, latent, main_outside, index_query, index_weights, index_keys, *rest)
    fits = (
        lax.axis_size("head") == GROUPS
        and lax.axis_size("seq") % 2 == 0
        and main_query.shape[0] == 128
        and main_outside.shape[1] % PER_STEP == 0
        and main_outside.shape[1] <= 128
        and latent.shape[0] % 256 == 0
        and latent.shape[1] == LAT
        and 3 * index_weights.shape[1] <= 128
        and index_weights.shape[1] % 16 == 0
    )
    return shards(*args) if fits else plain_shards(*args)


def solution(mesh):
    in_specs = (
        P("seq", "head"),
        P("seq", None),
        P("seq", "head"),
        P("seq", "head"),
        P("seq", "head"),
        P("seq", None),
        P("seq"),
        P("seq"),
        P("seq"),
    )
    out_specs = (P("seq", "head"), P("seq", "head"), P("seq", None))
    return jax.shard_map(any_shards, mesh=mesh, in_specs=in_specs, out_specs=out_specs, check_vma=False)
```

```python
import functools

import jax
import jax.numpy as jnp
from jax import lax
from jax.experimental import pallas as pl
from jax.experimental.pallas import tpu as pltpu
from jax.sharding import PartitionSpec as P

IDIM = 128
KB = 256
STEPS = 4


NEGATIVE = -1e30
SCORE_SCALE = 192.0 ** (-0.5)


def passed_along(block, axis, distance):
    devices = range(lax.axis_size(axis))
    route = [(i - distance, i) for i in devices if i - distance in devices]
    return lax.ppermute(block, axis, route)


def head_mass(scores, visible, outside):
    masked = jnp.where(visible[None], scores, NEGATIVE)
    highest = jnp.maximum(jnp.max(masked, axis=2), outside.T)
    expo = jnp.exp(masked - highest[:, :, None])
    total = jnp.sum(expo, axis=2) + jnp.exp(outside.T - highest)
    return jnp.sum(expo / total[:, :, None], axis=0)


def score_grad(mass, index_score, visible, outside):
    target = mass / jnp.sum(mass, axis=1, keepdims=True)
    masked = jnp.where(visible, index_score, NEGATIVE)
    highest = jnp.maximum(jnp.max(masked, axis=1), outside)
    expo = jnp.exp(masked - highest[:, None])
    total = jnp.sum(expo, axis=1) + jnp.exp(outside - highest)
    return (expo / total[:, None] - target) * (STEPS * KB)


def plain_shards(
    main_query,
    latent,
    main_outside,
    index_query,
    index_weights,
    index_keys,
    index_outside,
    query_pos,
    key_pos,
):
    query_rows = main_query.shape[0]
    block_keys = latent.shape[0]
    width = latent.shape[1]
    local_heads = main_outside.shape[1]
    local_index = index_weights.shape[1]
    index_width = index_keys.shape[1]
    window = STEPS * block_keys
    factor = IDIM ** (-0.5)
    position = lax.axis_index("seq")
    latent_parts = []
    index_parts = []
    for distance in range(STEPS - 1, 0, -1):
        latent_parts.append(passed_along(latent, "seq", distance))
        index_parts.append(passed_along(index_keys, "seq", distance))
    latent_window = jnp.concatenate(latent_parts + [latent], 0)
    key_window = jnp.concatenate(index_parts + [index_keys], 0)
    slot_block = jnp.arange(window, dtype=jnp.int32) // block_keys
    lagging = STEPS - 1 - slot_block
    places_full = jnp.concatenate([jnp.zeros((window - block_keys,), jnp.int32), key_pos], 0)
    causal = (slot_block < STEPS - 1)[None, :] | (places_full[None, :] <= query_pos[:, None])
    visible = (position >= lagging)[None, :] & causal
    queries = main_query.reshape(query_rows, local_heads, width)
    scores = (
        jnp.einsum("qhc,wc->hqw", queries, latent_window, preferred_element_type=jnp.float32)
        * SCORE_SCALE
    )
    mass_part = head_mass(scores, visible, main_outside)
    index_rows = index_query.reshape(query_rows, local_index, index_width)
    activity = (
        jnp.einsum("qjd,wd->jqw", index_rows, key_window, preferred_element_type=jnp.float32)
        * factor
    )
    rectified = jnp.maximum(activity, 0.0)
    index_part = jnp.einsum("qj,jqw->qw", index_weights, rectified)
    mass, index_score = (
        lax.psum_scatter(mass_part, "head", scatter_dimension=0, tiled=True),
        lax.psum_scatter(index_part, "head", scatter_dimension=0, tiled=True),
    )
    share = mass.shape[0]
    start = lax.axis_index("head") * share
    visible_rows = lax.dynamic_slice_in_dim(visible, start, share, 0)
    outside_rows = lax.dynamic_slice_in_dim(index_outside, start, share, 0)
    dscore = lax.all_gather(
        score_grad(mass, index_score, visible_rows, outside_rows), "head", axis=0, tiled=True
    )
    gated = dscore[None] * index_weights.T[:, :, None] * (activity > 0).astype(jnp.float32)
    key_wide = key_window.astype(jnp.float32)
    rows_wide = index_rows.astype(jnp.float32)
    grad_query = (
        jnp.einsum("jqw,wd->qjd", gated, key_wide, precision=lax.Precision.HIGHEST) * factor
    )
    grad_query = grad_query.astype(jnp.bfloat16).reshape(query_rows, local_index * index_width)
    grad_weight = jnp.einsum("qw,jqw->qj", dscore, rectified)
    grad_window = (
        jnp.einsum("jqw,qjd->wd", gated, rows_wide, precision=lax.Precision.HIGHEST) * factor
    )
    grad_parts = grad_window.reshape(STEPS, block_keys, index_width)
    grad_total = grad_parts[STEPS - 1]
    for distance in range(1, STEPS):
        grad_total = grad_total + passed_along(grad_parts[STEPS - 1 - distance], "seq", -distance)
    grad_keys = lax.psum(grad_total, "head")
    return (grad_query, grad_weight, grad_keys)


LOG2E = 1.4426950408889634
LAT = 576
GROUPS = 4
BUFFERS = 4
PER_STEP = 8
SAFE = 1e30
LEVELS = 32000.0
NN = (((1,), (0,)), ((), ()))
NT = (((1,), (1,)), ((), ()))


def dot(a, b, dims=NN):
    return lax.dot_general(a, b, dims, preferred_element_type=jnp.float32)


def split(x):
    high = x.astype(jnp.bfloat16)
    return high, (x - high.astype(jnp.float32)).astype(jnp.bfloat16)


def coded(x, axis):
    top = jnp.max(jnp.abs(x), axis=axis, keepdims=True)
    power = jnp.ceil(8.0 * jnp.log2(jnp.maximum(top, 1e-30)))
    code = jnp.floor(x * (LEVELS * jnp.exp2(power * -0.125)) + 0.5)
    return code.astype(jnp.int32).astype(jnp.int16), power.astype(jnp.int32).astype(jnp.int16)


def scale_of(power):
    return jnp.exp2(power.astype(jnp.float32) * 0.125) * (1.0 / LEVELS)


def coded_rows(ref, x):
    code, power = coded(x, 1)
    ref[:, :x.shape[1]] = code
    ref[:, x.shape[1]:] = jnp.broadcast_to(power.astype(jnp.int32), (x.shape[0], 128)).astype(jnp.int16)


def restored_rows(ref, window):
    return ref[:, :window].astype(jnp.float32) * scale_of(ref[:, window:])[:, :1]


def coded_columns(ref, x):
    code, power = coded(x, 0)
    ref[:x.shape[0], :] = code
    ref[x.shape[0]:, :] = jnp.broadcast_to(power.astype(jnp.int32), (16, x.shape[1])).astype(jnp.int16)


def restored_columns(ref, count):
    return ref[:count, :].astype(jnp.float32) * scale_of(ref[count:, :])[:1, :]


def column(row, first, count):
    lane = lax.broadcasted_iota(jnp.int32, (count, 128), 1)
    line = lax.broadcasted_iota(jnp.int32, (count, 128), 0) + first
    wide = jnp.broadcast_to(row.astype(jnp.float32), (count, 128))
    return jnp.sum(jnp.where(lane == line, wide, 0.0), axis=1, keepdims=True)


def turned_tall(x, value=0.0):
    fill = jnp.full((128 - x.shape[0], 128), value, jnp.float32)
    return jnp.concatenate([x, fill], 0).T


def slots_of(position):
    even = lax.rem(position, 2) == 0
    return 3, jnp.where(even, 0, 2), jnp.where(even, 2, 0), 1


def gathered(position, blocks, kept):
    kb = blocks[0].shape[1]
    for block, slot in zip(blocks, slots_of(position)):
        at = pl.ds(pl.multiple_of(slot * kb, kb), kb)
        kept[:, at] = block[block.shape[0] - IDIM:, :]


def pack_kernel(place, latent, keys, query, weight, packed, turned_keys, *rest):
    outs, (kept, weight_here, keys_here, sems) = rest[:GROUPS], rest[GROUPS:]
    share = outs[0].shape[0]
    width, count = query.shape[1], weight.shape[0]
    copies = [
        pltpu.make_async_copy(weight, weight_here, sems.at[GROUPS]),
        pltpu.make_async_copy(keys, keys_here, sems.at[GROUPS + 1]),
        pltpu.make_async_copy(latent, packed.at[pl.ds(0, LAT), :], sems.at[GROUPS + 2]),
    ]
    for d in range(GROUPS):
        at = pl.ds(pl.multiple_of((place[0] ^ d) * share, share), share)
        here = outs[d].at[:, pl.ds(0, width)]
        copies.append(pltpu.make_async_copy(query.at[at, :], here, sems.at[d]))
    for copy in copies:
        copy.start()
    copies[1].wait()
    turned = keys_here[...].T
    packed[LAT:, :] = turned
    turned_keys[...] = turned
    copies[0].wait()
    tall = turned_tall(weight_here[...])[:, :count]
    high = tall.astype(jnp.bfloat16)
    middle, low = split(tall - high.astype(jnp.float32))
    kept[...] = jnp.concatenate([high, middle, low, jnp.zeros((128, 128 - 3 * count), jnp.bfloat16)], 1)
    for d in range(GROUPS):
        at = pl.ds(pl.multiple_of((place[0] ^ d) * share, share), share)
        outs[d][:, width:] = kept[at, :]
    for copy in copies[2:]:
        copy.wait()


def weights_of(piece, width, count):
    tail = piece[:, width:].astype(jnp.float32)
    return tail[:, :count] + tail[:, count:2 * count] + tail[:, 2 * count:3 * count]


def chunk_rows(q, j, half):
    parity, pair = j % 2, half * (j // 2)
    starts = [1152 * (pair + i) + 512 * parity for i in range(half)]
    return jnp.concatenate([q[:, s:s + 640] for s in starts], 0), 64 - 64 * parity


def own_kernel(half, q, own, qpos, kpos, out, keys, here, places, sems):
    rows, kb = q.shape[0], own.shape[1]
    chunks = q.shape[1] // (half * LAT)
    parts = chunks // 2
    copies = [
        pltpu.make_async_copy(qpos, places.at[0:1, pl.ds(0, rows)], sems.at[parts]),
        pltpu.make_async_copy(kpos, places.at[1:2, :], sems.at[parts + 1]),
    ]
    for i in range(parts):
        lanes = pl.ds(i * 2 * half * LAT, 2 * half * LAT)
        copies.append(pltpu.make_async_copy(q.at[:, lanes], here.at[:, lanes], sems.at[i]))
    for copy in copies:
        copy.start()
    keys[:64, :] = jnp.zeros((64, kb), jnp.bfloat16)
    keys[64:64 + LAT, :] = own[:LAT, :]
    keys[64 + LAT:, :] = jnp.zeros((64, kb), jnp.bfloat16)
    copies[0].wait()
    copies[1].wait()
    causal = places[1:2, :].astype(jnp.float32) <= column(places[0:1, :rows], 0, rows)
    for j in range(chunks):
        if j % 2 == 0:
            copies[2 + j // 2].wait()
        lhs, first = chunk_rows(here, j, half)
        s = dot(lhs, keys[first:first + 640, :])
        for i in range(half):
            ex = jnp.exp2(s[i * rows:(i + 1) * rows] * (SCORE_SCALE * LOG2E))
            at = (j * half + i) * rows
            out[at:at + rows, :] = jnp.where(causal, ex, 0.0)


def block_kernel(half, q, block, out, keys):
    rows, kb = q.shape[0], block.shape[1]
    keys[:64, :] = jnp.zeros((64, kb), jnp.bfloat16)
    keys[64:64 + LAT, :] = block[:LAT, :]
    keys[64 + LAT:, :] = jnp.zeros((64, kb), jnp.bfloat16)
    size = half * rows
    for j in range(q.shape[1] // (half * LAT)):
        lhs, first = chunk_rows(q, j, half)
        out[j * size:(j + 1) * size, :] = jnp.exp2(dot(lhs, keys[first:first + 640, :]) * (SCORE_SCALE * LOG2E))


def main_kernel(half, place, q, own, a, b, c, own_exp, b_exp, outside, qpos, kpos, *rest):
    outs, rest = rest[:GROUPS], rest[GROUPS:]
    e, inv, (keys, out_exp, mass) = rest[:BUFFERS], rest[BUFFERS:2 * BUFFERS], rest[2 * BUFFERS:]
    z, position = place[0], place[1]
    rows, kb = q.shape[0], own.shape[1]
    chunks = q.shape[1] // (half * LAT)
    window = STEPS * kb
    own_slot, a_slot, b_slot, c_slot = slots_of(position)
    slots = (a_slot, c_slot, b_slot, own_slot)
    present = [position >= STEPS - 1 - slot for slot in slots]
    later = 2
    done = {later: b_exp, later + 1: own_exp}
    lane = lax.broadcasted_iota(jnp.int32, (32, 128), 1)

    keys[:64, :] = jnp.zeros((64, window), jnp.bfloat16)
    keys[64 + LAT:, :] = jnp.zeros((64, window), jnp.bfloat16)
    for i, block in enumerate((a, c)):
        keys[64:64 + LAT, i * kb:(i + 1) * kb] = block[:LAT, :]
    out_exp[...] = jnp.exp(turned_tall(outside[...], NEGATIVE))
    mass[...] = jnp.zeros_like(mass)
    worst = [jnp.zeros((32, 1), jnp.float32)]

    def exp_unit(j, i, r):
        buffer, at = j % BUFFERS, i * rows + r
        done_rows = slice(j * half * rows + at, j * half * rows + at + 32)
        head = (j - j % 2) * half + 2 * i + j % 2
        total = jnp.where(lane == head, out_exp[r:r + 32, :], 0.0)
        for block in range(STEPS):
            if block in done:
                piece = done[block][done_rows, :]
            else:
                piece = e[buffer][at:at + 32, block * kb:(block + 1) * kb]
            sums = piece[:, :128]
            for k in range(128, kb, 128):
                sums = sums + piece[:, k:k + 128]
            total = total + (sums if block == STEPS - 1 else jnp.where(present[block], sums, 0.0))
        total = jnp.sum(total, axis=1, keepdims=True)
        inv[buffer][at:at + 32, :] = jnp.broadcast_to(1.0 / total, (32, 128))
        worst[0] = jnp.maximum(worst[0], total)

    def mass_unit(j, r, w):
        buffer = j % BUFFERS
        total = mass[r:r + 32, w:w + 2 * kb]
        for i in range(half):
            at = i * rows + r
            if w // kb in done:
                first = j * half * rows + at
                piece = jnp.concatenate([done[w // kb + k][first:first + 32, :] for k in range(2)], 1)
            else:
                piece = e[buffer][at:at + 32, :]
            scale = inv[buffer][at:at + 32, :]
            total = total + piece * jnp.concatenate([scale] * (2 * kb // 128), 1)
        mass[r:r + 32, w:w + 2 * kb] = total

    exps = [(i, r) for i in range(half) for r in range(0, rows, 32)]
    sums = [(r, w) for r in range(0, rows, 32) for w in range(0, window, 2 * kb)]
    thirds = later
    for j in range(chunks + 2):
        if j < chunks:
            lhs, first = chunk_rows(q, j, half)
        for n in range(thirds):
            if j < chunks:
                lanes = slice(n * kb, (n + 1) * kb)
                s = dot(lhs, keys[first:first + 640, lanes])
                e[j % BUFFERS][:, lanes] = jnp.exp2(s * (SCORE_SCALE * LOG2E))
            if 1 <= j <= chunks:
                for i, r in exps[n * len(exps) // thirds:(n + 1) * len(exps) // thirds]:
                    exp_unit(j - 1, i, r)
            if j >= 2:
                for r, w in sums[n * len(sums) // thirds:(n + 1) * len(sums) // thirds]:
                    mass_unit(j - 2, r, w)

    @pl.when(jnp.logical_not(jnp.max(worst[0]) < SAFE))
    def _():
        for i, block in enumerate((b, own)):
            keys[64:64 + LAT, (later + i) * kb:(later + i + 1) * kb] = block[:LAT, :]
        causal = kpos[...].astype(jnp.float32) <= column(qpos[...], 0, rows)
        seen = [jnp.where(p, jnp.ones((rows, kb), jnp.float32), 0.0) for p in present[:STEPS - 1]]
        visible = jnp.concatenate(seen + [jnp.where(causal, 1.0, 0.0)], 1) > 0
        line = lax.broadcasted_iota(jnp.int32, outside.shape, 0)
        mass[...] = jnp.zeros_like(mass)
        for parity in range(2):

            def exact(i, carry, parity=parity):
                first = 64 - 64 * parity
                at = pl.multiple_of(1152 * i + 512 * parity, 128)
                scores = dot(q[:, pl.ds(at, 640)], keys[first:first + 640, :]) * SCORE_SCALE
                masked = jnp.where(visible, scores, NEGATIVE)
                mine = jnp.sum(jnp.where(line == 2 * i + parity, outside[...], 0.0), axis=0, keepdims=True)
                mine = column(mine, 0, rows)
                top = jnp.maximum(jnp.max(masked, axis=1, keepdims=True), mine)
                ex = jnp.exp(masked - top)
                total = jnp.sum(ex, axis=1, keepdims=True) + jnp.exp(mine - top)
                mass[...] += ex * (1.0 / total)
                return carry

            lax.fori_loop(0, outside.shape[0] // 2, exact, 0)

    ordered = [mass[:, i * kb:(i + 1) * kb] for i in range(STEPS)]
    ordered = [x if i == STEPS - 1 else jnp.where(present[i], x, 0.0) for i, x in enumerate(ordered)]
    for slot, x in zip(slots, ordered):
        mass[:, pl.ds(pl.multiple_of(slot * kb, kb), kb)] = x
    share = rows // GROUPS
    for d in range(GROUPS):
        at = pl.ds(pl.multiple_of((z ^ d) * share, share), share)
        if d == 0:
            outs[d][...] = mass[at, :]
        else:
            coded_rows(outs[d], mass[at, :])


def heads_of(piece, count):
    return jnp.concatenate([piece[:, IDIM * j:IDIM * (j + 1)] for j in range(count)], 0)


def index_kernel(count, place, own, a, b, c, *rest):
    pieces, (score, gate, turned, keys) = rest[:GROUPS], rest[GROUPS:]
    share = score.shape[0]
    tile = count * share
    gathered(place[1], (own, a, b, c), keys)
    total = jnp.zeros(score.shape, jnp.float32)
    for d in range(GROUPS):
        piece = pieces[d][...]
        scaled = weights_of(piece, IDIM * count, count) * (IDIM ** -0.5)
        rows = heads_of(piece, count)
        act = dot(rows, keys[...])
        gate[d * tile:(d + 1) * tile, :] = jnp.where(act > 0, 1.0, 0.0).astype(jnp.bfloat16)
        for j in range(count):
            total = total + jnp.maximum(act[j * share:(j + 1) * share], 0.0) * scaled[:, j:j + 1]
        tall = jnp.concatenate([jnp.broadcast_to(scaled[:, j:j + 1], (share, IDIM)) for j in range(count)], 0)
        high, low = split(rows.astype(jnp.float32) * tall)
        turned[:IDIM, d * tile:(d + 1) * tile] = high.T
        turned[IDIM:, d * tile:(d + 1) * tile] = low.T
    score[...] = total


def dscore_kernel(place, m0, m3, m2, m1, score, outside, qpos, kpos, spread, code):
    z, position = place[0], place[1]
    share, window = score.shape
    kb = kpos.shape[1]
    mass = (m0[...] + restored_rows(m1, window)) + (restored_rows(m2, window) + restored_rows(m3, window))
    target = mass / jnp.sum(mass, axis=1, keepdims=True)
    slot = lax.broadcasted_iota(jnp.int32, (share, window), 1) // kb
    causal = kpos[...].astype(jnp.float32) <= column(qpos[...], z * share, share)
    masked = jnp.where(position >= STEPS - 1 - slot, score[...], NEGATIVE)
    masked = jnp.concatenate([masked[:, :window - kb], jnp.where(causal, masked[:, window - kb:], NEGATIVE)], 1)
    out = column(outside[...], z * share, share)
    top = jnp.maximum(jnp.max(masked, axis=1, keepdims=True), out)
    expo = jnp.exp(masked - top)
    total = jnp.sum(expo, axis=1, keepdims=True) + jnp.exp(out - top)
    dscore = (expo / total - target) * float(window)
    spread[0], spread[1] = split(dscore)
    coded_rows(code, dscore)


def keys_kernel(count, gate, turned, spread, *outs):
    tile = count * spread.shape[1]
    total = None
    for d in range(GROUPS):
        rows = slice(d * tile, (d + 1) * tile)
        mask = gate[rows, :]
        both = dot(turned[:, rows], mask * jnp.concatenate([spread[0]] * count, 0))
        low = dot(turned[:IDIM, rows], mask * jnp.concatenate([spread[1]] * count, 0))
        part = both[:IDIM] + both[IDIM:] + low
        total = part if total is None else total + part
    kb = outs[STEPS - 1].shape[0]
    for i in range(STEPS):
        part = total[:, i * kb:(i + 1) * kb].T
        if i < STEPS - 1:
            coded_columns(outs[i], part)
        else:
            outs[i][...] = part


def query_kernel(heads, group, place, own, a, b, c, query, weight, c0, c1, c2, c3, *rest):
    first = heads[0]
    if first:
        (done, before), rest = rest[:2], rest[2:]
    grad, out, keys, turned, high, low, scale, tall = rest
    share, rows = c0.shape[0], query.shape[0]
    window = keys.shape[1]
    gathered(place[1], (own, a, b, c), keys)
    turned[...] = keys[...].T
    for d, code in enumerate((c0, c1, c2, c3)):
        at = pl.ds(pl.multiple_of((place[0] ^ d) * share, share), share)
        high[at, :], low[at, :] = split(code[:, :window].astype(jnp.float32))
        scale[at, :] = scale_of(code[:, window:]) * (IDIM ** -0.5)
    tall[...] = turned_tall(weight[...])
    lane = lax.broadcasted_iota(jnp.int32, (rows, 128), 1)
    total = before[...] if first else jnp.zeros((rows, 128), jnp.float32)
    if first:
        grad[:, :IDIM * first] = done[:, :IDIM * first]
    for g in range(*heads, group):
        tile = heads_of(query[:, IDIM * g:IDIM * (g + group)], group)
        mask = jnp.where(dot(tile, keys[...]) > 0, 1.0, 0.0).astype(jnp.bfloat16)
        part = dot(mask * jnp.concatenate([high[...]] * group, 0), turned[...])
        part = part + dot(mask * jnp.concatenate([low[...]] * group, 0), turned[...])
        for j in range(g, g + group):
            lanes = slice(IDIM * j, IDIM * (j + 1))
            mine = part[(j - g) * rows:(j - g + 1) * rows] * scale[...]
            grad[:, lanes] = (mine * tall[:, j:j + 1]).astype(jnp.bfloat16)
            product = jnp.sum(mine * query[:, lanes].astype(jnp.float32), axis=1, keepdims=True)
            total = jnp.where(lane == j, product, total)
    out[...] = total.T[:out.shape[0], :] if first else total


def owned_kernel(p0, c1, c2, c3, after, code):
    kb = p0.shape[0]
    moved = [restored_columns(c, kb) for c in (c1, c2, c3)]
    coded_columns(code, (p0[...] + moved[0]) + (moved[1] + moved[2]))


def total_kernel(c0, c1, c2, c3, out):
    parts = [restored_columns(c, out.shape[0]) for c in (c0, c1, c2, c3)]
    out[...] = (parts[0] + parts[1]) + (parts[2] + parts[3])


SMEM = pl.BlockSpec(memory_space=pltpu.SMEM)
HBM = pl.BlockSpec(memory_space=pltpu.HBM)


def held(array):
    return pltpu.with_memory_space_constraint(array, pltpu.HBM)


def whole(array):
    rank = len(array.shape)
    return pl.BlockSpec(array.shape, lambda i: (0,) * rank)


def params(mib):
    return pltpu.CompilerParams(vmem_limit_bytes=mib << 20)


def cost(flops, size):
    return pl.CostEstimate(flops=1, bytes_accessed=1, transcendentals=0)


def along(x, axis, route):
    size = lax.axis_size(axis)
    return lax.ppermute(x, axis, [(i, j % size) for i, j in route])


def shards(
    main_query,
    latent,
    main_outside,
    index_query,
    index_weights,
    index_keys,
    index_outside,
    query_pos,
    key_pos,
):
    rows = main_query.shape[0]
    kb = latent.shape[0]
    heads = main_outside.shape[1]
    count = index_weights.shape[1]
    share = rows // GROUPS
    window = STEPS * kb
    n_seq = lax.axis_size("seq")
    z, position = lax.axis_index("head"), lax.axis_index("seq")
    place = jnp.stack([z, position]).astype(jnp.int32)
    bf16, f32, int16 = jnp.bfloat16, jnp.float32, jnp.int16

    def shape(dims, kind):
        return jax.ShapeDtypeStruct(dims, kind)

    def exchanged(x, d):
        return along(x, "head", [(i, i ^ d) for i in range(GROUPS)])

    weights = index_weights.T
    outsides = main_outside.T
    qpos = query_pos.reshape(1, rows)
    kpos = key_pos.reshape(1, kb)
    outside = index_outside.reshape(1, rows)
    piece_shape = (share, IDIM * count + 128)
    packed = latent.T
    to_b = [(i, i + (3 if i % 2 == 0 else 1)) for i in range(n_seq)]
    to_a = [(i, i + (1 if i % 2 == 0 else 3)) for i in range(n_seq)]
    to_c = [(i, i ^ 1) for i in range(n_seq)]
    route_b = along(packed, "seq", to_b)
    turned_shape = (IDIM, kb)
    both_shape = (LAT + IDIM, kb)
    both, turned_keys, *mine = pl.pallas_call(
        pack_kernel,
        grid=(1,),
        in_specs=[SMEM] + [HBM] * 4,
        out_specs=[pl.BlockSpec(both_shape, lambda i: (0, 0)), pl.BlockSpec(turned_shape, lambda i: (0, 0))]
        + [pl.BlockSpec(piece_shape, lambda i: (0, 0))] * GROUPS,
        out_shape=[shape(both_shape, bf16), shape(turned_shape, bf16)] + [shape(piece_shape, bf16)] * GROUPS,
        scratch_shapes=[
            pltpu.VMEM((rows, 128), bf16),
            pltpu.VMEM((count, rows), f32),
            pltpu.VMEM((kb, IDIM), bf16),
            pltpu.SemaphoreType.DMA((GROUPS + 3,)),
        ],
        compiler_params=params(16),
        cost_estimate=cost(0, 4 * rows * count * IDIM),
        name="pack_rows",
    )(place, *[held(x) for x in (packed, index_keys, index_query, weights)])
    route_a = along(both, "seq", to_a)
    pieces = [mine[0]] + [exchanged(mine[d], d) for d in range(1, GROUPS)]

    half = PER_STEP // 2
    own_exp = pl.pallas_call(
        functools.partial(own_kernel, half),
        grid=(1,),
        in_specs=[HBM, whole(packed), HBM, HBM],
        out_specs=pl.BlockSpec((heads * rows, kb), lambda i: (0, 0)),
        out_shape=shape((heads * rows, kb), f32),
        scratch_shapes=[
            pltpu.VMEM((704, kb), bf16),
            pltpu.VMEM(main_query.shape, bf16),
            pltpu.VMEM((8, kb), jnp.int32),
            pltpu.SemaphoreType.DMA((heads // PER_STEP + 2,)),
        ],
        compiler_params=params(24),
        cost_estimate=cost(2 * heads * rows * kb * LAT, heads * rows * (2 * LAT + 4 * kb)),
        name="own_block",
    )(held(main_query), packed, held(qpos), held(kpos))

    route_b, own_exp, pieces[1] = lax.optimization_barrier((route_b, own_exp, pieces[1]))
    b_exp = pl.pallas_call(
        functools.partial(block_kernel, half),
        grid=(1,),
        in_specs=[whole(main_query), whole(route_b)],
        out_specs=pl.BlockSpec((heads * rows, kb), lambda i: (0, 0)),
        out_shape=shape((heads * rows, kb), f32),
        scratch_shapes=[pltpu.VMEM((704, kb), bf16)],
        compiler_params=params(16),
        cost_estimate=cost(2 * heads * rows * kb * LAT, heads * rows * (2 * LAT + 4 * kb)),
        name="next_block",
    )(main_query, route_b)
    route_c = along(route_b, "seq", to_c)
    blocks = (packed, route_a, route_b, route_c)
    sent_keys, b_exp = lax.optimization_barrier((turned_keys, b_exp))
    keys_b = along(sent_keys, "seq", to_b)
    key_rows = (turned_keys, route_a, keys_b, along(keys_b, "seq", to_c))
    code_shape = (share, window + 128)
    mass = pl.pallas_call(
        functools.partial(main_kernel, half),
        grid=(1,),
        in_specs=[SMEM] + [whole(x) for x in (main_query, *blocks, own_exp, b_exp, outsides, qpos, kpos)],
        out_specs=[pl.BlockSpec((share, window), lambda i: (0, 0))]
        + [pl.BlockSpec(code_shape, lambda i: (0, 0))] * (GROUPS - 1),
        out_shape=[shape((share, window), f32)] + [shape(code_shape, int16)] * (GROUPS - 1),
        scratch_shapes=[pltpu.VMEM((half * rows, 2 * kb), f32)] * BUFFERS
        + [pltpu.VMEM((half * rows, 128), f32)] * BUFFERS
        + [
            pltpu.VMEM((704, window), bf16),
            pltpu.VMEM((rows, 128), f32),
            pltpu.VMEM((rows, window), f32),
        ],
        compiler_params=params(32),
        cost_estimate=cost(2 * heads * rows * window * LAT, heads * rows * 2 * LAT),
        name="main_mass",
    )(place, main_query, *blocks, own_exp, b_exp, outsides, qpos, kpos)
    masses = [mass[0]] + [exchanged(mass[d], d) for d in range(1, GROUPS)]

    tile = count * share
    score, gate, turned = pl.pallas_call(
        functools.partial(index_kernel, count),
        grid=(1,),
        in_specs=[SMEM] + [whole(x) for x in key_rows] + [whole(x) for x in pieces],
        out_specs=[
            pl.BlockSpec((share, window), lambda i: (0, 0)),
            pl.BlockSpec((GROUPS * tile, window), lambda i: (0, 0)),
            pl.BlockSpec((2 * IDIM, GROUPS * tile), lambda i: (0, 0)),
        ],
        out_shape=[
            shape((share, window), f32),
            shape((GROUPS * tile, window), bf16),
            shape((2 * IDIM, GROUPS * tile), bf16),
        ],
        scratch_shapes=[pltpu.VMEM((IDIM, window), bf16)],
        compiler_params=params(24),
        cost_estimate=cost(4 * GROUPS * tile * window * IDIM, GROUPS * tile * window * 2),
        name="index_scores",
    )(place, *key_rows, *pieces)

    spread, code = pl.pallas_call(
        dscore_kernel,
        grid=(1,),
        in_specs=[SMEM] + [whole(x) for x in (masses[0], *masses[:0:-1], score, outside, qpos, kpos)],
        out_specs=[
            pl.BlockSpec((2, share, window), lambda i: (0, 0, 0)),
            pl.BlockSpec(code_shape, lambda i: (0, 0)),
        ],
        out_shape=[shape((2, share, window), bf16), shape(code_shape, int16)],
        compiler_params=params(16),
        cost_estimate=cost(0, 12 * share * window),
        name="dscores",
    )(place, masses[0], *masses[:0:-1], score, outside, qpos, kpos)
    codes = [code] + [exchanged(code, d) for d in range(1, GROUPS)]

    sum_shape = (kb + 16, IDIM)
    parts = pl.pallas_call(
        functools.partial(keys_kernel, count),
        grid=(1,),
        in_specs=[whole(gate), whole(turned), whole(spread)],
        out_specs=[pl.BlockSpec(sum_shape, lambda i: (0, 0))] * (STEPS - 1)
        + [pl.BlockSpec((kb, IDIM), lambda i: (0, 0))],
        out_shape=[shape(sum_shape, int16)] * (STEPS - 1) + [shape((kb, IDIM), f32)],
        compiler_params=params(24),
        cost_estimate=cost(8 * GROUPS * tile * window * IDIM, GROUPS * tile * window * 2),
        name="key_grads",
    )(gate, turned, spread)
    sent = [parts[STEPS - 1 - distance] for distance in range(1, STEPS)]
    sent[-1], codes[2] = lax.optimization_barrier((sent[-1], codes[2]))
    moved = [along(x, "seq", [(i, i - d - 1) for i in range(n_seq)]) for d, x in enumerate(sent)]

    group = count // 4

    def query_grads(first, last, before):
        sums_shape = (count, rows) if first else (rows, 128)
        return pl.pallas_call(
            functools.partial(query_kernel, (first, last), group),
            grid=(1,),
            in_specs=[SMEM] + [whole(x) for x in key_rows]
            + [whole(x) for x in (index_query, weights, *codes)]
            + [whole(x) for x in before],
            out_specs=[
                pl.BlockSpec((rows, IDIM * count), lambda i: (0, 0)),
                pl.BlockSpec(sums_shape, lambda i: (0, 0)),
            ],
            out_shape=[shape((rows, IDIM * count), bf16), shape(sums_shape, f32)],
            scratch_shapes=[
                pltpu.VMEM((IDIM, window), bf16),
                pltpu.VMEM((window, IDIM), bf16),
                pltpu.VMEM((rows, window), bf16),
                pltpu.VMEM((rows, window), bf16),
                pltpu.VMEM((rows, 128), f32),
                pltpu.VMEM((rows, 128), f32),
            ],
            compiler_params=params(24),
            cost_estimate=cost(8 * rows * (last - first) * window * IDIM, 8 * rows * count * IDIM),
            name="query_grads",
        )(place, *key_rows, index_query, weights, *codes, *before)

    begun = query_grads(0, group, ())
    grad_query, grad_weight = query_grads(group, count, begun)

    owned = pl.pallas_call(
        owned_kernel,
        grid=(1,),
        in_specs=[whole(x) for x in (parts[STEPS - 1], *moved, begun[1])],
        out_specs=pl.BlockSpec(sum_shape, lambda i: (0, 0)),
        out_shape=shape(sum_shape, int16),
        compiler_params=params(16),
        cost_estimate=cost(0, 20 * kb * IDIM),
        name="owned_keys",
    )(parts[STEPS - 1], *moved, begun[1])
    owners = [owned] + [exchanged(owned, d) for d in range(1, GROUPS)]
    grad_keys = pl.pallas_call(
        total_kernel,
        grid=(1,),
        in_specs=[whole(x) for x in owners],
        out_specs=pl.BlockSpec((kb, IDIM), lambda i: (0, 0)),
        out_shape=shape((kb, IDIM), f32),
        compiler_params=params(16),
        cost_estimate=cost(0, 12 * kb * IDIM),
        name="total_keys",
    )(*owners)
    return (grad_query, grad_weight.T, grad_keys)


def any_shards(main_query, latent, main_outside, index_query, index_weights, index_keys, *rest):
    args = (main_query, latent, main_outside, index_query, index_weights, index_keys, *rest)
    fits = (
        lax.axis_size("head") == GROUPS
        and lax.axis_size("seq") % 2 == 0
        and main_query.shape[0] == 128
        and main_outside.shape[1] % PER_STEP == 0
        and main_outside.shape[1] <= 128
        and latent.shape[0] % 256 == 0
        and latent.shape[1] == LAT
        and 3 * index_weights.shape[1] <= 128
        and index_weights.shape[1] % 16 == 0
    )
    return shards(*args) if fits else plain_shards(*args)


def solution(mesh):
    in_specs = (
        P("seq", "head"),
        P("seq", None),
        P("seq", "head"),
        P("seq", "head"),
        P("seq", "head"),
        P("seq", None),
        P("seq"),
        P("seq"),
        P("seq"),
    )
    out_specs = (P("seq", "head"), P("seq", "head"), P("seq", None))
    return jax.shard_map(any_shards, mesh=mesh, in_specs=in_specs, out_specs=out_specs, check_vma=False)
```

```python
import functools

import jax
import jax.numpy as jnp
from jax import lax
from jax.experimental import pallas as pl
from jax.experimental.pallas import tpu as pltpu
from jax.sharding import PartitionSpec as P

IDIM = 128
KB = 256
STEPS = 4


NEGATIVE = -1e30
SCORE_SCALE = 192.0 ** (-0.5)


def passed_along(block, axis, distance):
    devices = range(lax.axis_size(axis))
    route = [(i - distance, i) for i in devices if i - distance in devices]
    return lax.ppermute(block, axis, route)


def head_mass(scores, visible, outside):
    masked = jnp.where(visible[None], scores, NEGATIVE)
    highest = jnp.maximum(jnp.max(masked, axis=2), outside.T)
    expo = jnp.exp(masked - highest[:, :, None])
    total = jnp.sum(expo, axis=2) + jnp.exp(outside.T - highest)
    return jnp.sum(expo / total[:, :, None], axis=0)


def score_grad(mass, index_score, visible, outside):
    target = mass / jnp.sum(mass, axis=1, keepdims=True)
    masked = jnp.where(visible, index_score, NEGATIVE)
    highest = jnp.maximum(jnp.max(masked, axis=1), outside)
    expo = jnp.exp(masked - highest[:, None])
    total = jnp.sum(expo, axis=1) + jnp.exp(outside - highest)
    return (expo / total[:, None] - target) * (STEPS * KB)


def plain_shards(
    main_query,
    latent,
    main_outside,
    index_query,
    index_weights,
    index_keys,
    index_outside,
    query_pos,
    key_pos,
):
    query_rows = main_query.shape[0]
    block_keys = latent.shape[0]
    width = latent.shape[1]
    local_heads = main_outside.shape[1]
    local_index = index_weights.shape[1]
    index_width = index_keys.shape[1]
    window = STEPS * block_keys
    factor = IDIM ** (-0.5)
    position = lax.axis_index("seq")
    latent_parts = []
    index_parts = []
    for distance in range(STEPS - 1, 0, -1):
        latent_parts.append(passed_along(latent, "seq", distance))
        index_parts.append(passed_along(index_keys, "seq", distance))
    latent_window = jnp.concatenate(latent_parts + [latent], 0)
    key_window = jnp.concatenate(index_parts + [index_keys], 0)
    slot_block = jnp.arange(window, dtype=jnp.int32) // block_keys
    lagging = STEPS - 1 - slot_block
    places_full = jnp.concatenate([jnp.zeros((window - block_keys,), jnp.int32), key_pos], 0)
    causal = (slot_block < STEPS - 1)[None, :] | (places_full[None, :] <= query_pos[:, None])
    visible = (position >= lagging)[None, :] & causal
    queries = main_query.reshape(query_rows, local_heads, width)
    scores = (
        jnp.einsum("qhc,wc->hqw", queries, latent_window, preferred_element_type=jnp.float32)
        * SCORE_SCALE
    )
    mass_part = head_mass(scores, visible, main_outside)
    index_rows = index_query.reshape(query_rows, local_index, index_width)
    activity = (
        jnp.einsum("qjd,wd->jqw", index_rows, key_window, preferred_element_type=jnp.float32)
        * factor
    )
    rectified = jnp.maximum(activity, 0.0)
    index_part = jnp.einsum("qj,jqw->qw", index_weights, rectified)
    mass, index_score = (
        lax.psum_scatter(mass_part, "head", scatter_dimension=0, tiled=True),
        lax.psum_scatter(index_part, "head", scatter_dimension=0, tiled=True),
    )
    share = mass.shape[0]
    start = lax.axis_index("head") * share
    visible_rows = lax.dynamic_slice_in_dim(visible, start, share, 0)
    outside_rows = lax.dynamic_slice_in_dim(index_outside, start, share, 0)
    dscore = lax.all_gather(
        score_grad(mass, index_score, visible_rows, outside_rows), "head", axis=0, tiled=True
    )
    gated = dscore[None] * index_weights.T[:, :, None] * (activity > 0).astype(jnp.float32)
    key_wide = key_window.astype(jnp.float32)
    rows_wide = index_rows.astype(jnp.float32)
    grad_query = (
        jnp.einsum("jqw,wd->qjd", gated, key_wide, precision=lax.Precision.HIGHEST) * factor
    )
    grad_query = grad_query.astype(jnp.bfloat16).reshape(query_rows, local_index * index_width)
    grad_weight = jnp.einsum("qw,jqw->qj", dscore, rectified)
    grad_window = (
        jnp.einsum("jqw,qjd->wd", gated, rows_wide, precision=lax.Precision.HIGHEST) * factor
    )
    grad_parts = grad_window.reshape(STEPS, block_keys, index_width)
    grad_total = grad_parts[STEPS - 1]
    for distance in range(1, STEPS):
        grad_total = grad_total + passed_along(grad_parts[STEPS - 1 - distance], "seq", -distance)
    grad_keys = lax.psum(grad_total, "head")
    return (grad_query, grad_weight, grad_keys)


LOG2E = 1.4426950408889634
LAT = 576
GROUPS = 4
BUFFERS = 4
PER_STEP = 8
SAFE = 1e30
LEVELS = 32000.0
NN = (((1,), (0,)), ((), ()))
NT = (((1,), (1,)), ((), ()))


def dot(a, b, dims=NN):
    return lax.dot_general(a, b, dims, preferred_element_type=jnp.float32)


def split(x):
    high = x.astype(jnp.bfloat16)
    return high, (x - high.astype(jnp.float32)).astype(jnp.bfloat16)


def coded(x, axis):
    top = jnp.max(jnp.abs(x), axis=axis, keepdims=True)
    power = jnp.ceil(8.0 * jnp.log2(jnp.maximum(top, 1e-30)))
    code = jnp.floor(x * (LEVELS * jnp.exp2(power * -0.125)) + 0.5)
    return code.astype(jnp.int32).astype(jnp.int16), power.astype(jnp.int32).astype(jnp.int16)


def scale_of(power):
    return jnp.exp2(power.astype(jnp.float32) * 0.125) * (1.0 / LEVELS)


def coded_rows(ref, x):
    code, power = coded(x, 1)
    ref[:, :x.shape[1]] = code
    ref[:, x.shape[1]:] = jnp.broadcast_to(power.astype(jnp.int32), (x.shape[0], 128)).astype(jnp.int16)


def restored_rows(ref, window):
    return ref[:, :window].astype(jnp.float32) * scale_of(ref[:, window:])[:, :1]


def coded_columns(ref, x):
    code, power = coded(x, 0)
    ref[:x.shape[0], :] = code
    ref[x.shape[0]:, :] = jnp.broadcast_to(power.astype(jnp.int32), (16, x.shape[1])).astype(jnp.int16)


def restored_columns(ref, count):
    return ref[:count, :].astype(jnp.float32) * scale_of(ref[count:, :])[:1, :]


def column(row, first, count):
    lane = lax.broadcasted_iota(jnp.int32, (count, 128), 1)
    line = lax.broadcasted_iota(jnp.int32, (count, 128), 0) + first
    wide = jnp.broadcast_to(row.astype(jnp.float32), (count, 128))
    return jnp.sum(jnp.where(lane == line, wide, 0.0), axis=1, keepdims=True)


def turned_tall(x, value=0.0):
    fill = jnp.full((128 - x.shape[0], 128), value, jnp.float32)
    return jnp.concatenate([x, fill], 0).T


def slots_of(position):
    even = lax.rem(position, 2) == 0
    return 3, jnp.where(even, 0, 2), jnp.where(even, 2, 0), 1


def gathered(position, blocks, kept):
    kb = blocks[0].shape[1]
    for block, slot in zip(blocks, slots_of(position)):
        at = pl.ds(pl.multiple_of(slot * kb, kb), kb)
        kept[:, at] = block[block.shape[0] - IDIM:, :]


def pack_kernel(place, latent, keys, query, weight, packed, turned_keys, *rest):
    outs, (kept, weight_here, keys_here, sems) = rest[:GROUPS], rest[GROUPS:]
    share = outs[0].shape[0]
    width, count = query.shape[1], weight.shape[0]
    copies = [
        pltpu.make_async_copy(weight, weight_here, sems.at[GROUPS]),
        pltpu.make_async_copy(keys, keys_here, sems.at[GROUPS + 1]),
        pltpu.make_async_copy(latent, packed.at[pl.ds(0, LAT), :], sems.at[GROUPS + 2]),
    ]
    for d in range(GROUPS):
        at = pl.ds(pl.multiple_of((place[0] ^ d) * share, share), share)
        here = outs[d].at[:, pl.ds(0, width)]
        copies.append(pltpu.make_async_copy(query.at[at, :], here, sems.at[d]))
    for copy in copies:
        copy.start()
    copies[1].wait()
    turned = keys_here[...].T
    packed[LAT:, :] = turned
    turned_keys[...] = turned
    copies[0].wait()
    tall = turned_tall(weight_here[...])[:, :count]
    high = tall.astype(jnp.bfloat16)
    middle, low = split(tall - high.astype(jnp.float32))
    kept[...] = jnp.concatenate([high, middle, low, jnp.zeros((128, 128 - 3 * count), jnp.bfloat16)], 1)
    for d in range(GROUPS):
        at = pl.ds(pl.multiple_of((place[0] ^ d) * share, share), share)
        outs[d][:, width:] = kept[at, :]
    for copy in copies[2:]:
        copy.wait()


def weights_of(piece, width, count):
    tail = piece[:, width:].astype(jnp.float32)
    return tail[:, :count] + tail[:, count:2 * count] + tail[:, 2 * count:3 * count]


def chunk_rows(q, j, half):
    parity, pair = j % 2, half * (j // 2)
    starts = [1152 * (pair + i) + 512 * parity for i in range(half)]
    return jnp.concatenate([q[:, s:s + 640] for s in starts], 0), 64 - 64 * parity


def own_kernel(half, q, own, qpos, kpos, out, keys, here, places, sems):
    rows, kb = q.shape[0], own.shape[1]
    chunks = q.shape[1] // (half * LAT)
    parts = chunks // 2
    copies = [
        pltpu.make_async_copy(qpos, places.at[0:1, pl.ds(0, rows)], sems.at[parts]),
        pltpu.make_async_copy(kpos, places.at[1:2, :], sems.at[parts + 1]),
    ]
    for i in range(parts):
        lanes = pl.ds(i * 2 * half * LAT, 2 * half * LAT)
        copies.append(pltpu.make_async_copy(q.at[:, lanes], here.at[:, lanes], sems.at[i]))
    for copy in copies:
        copy.start()
    keys[:64, :] = jnp.zeros((64, kb), jnp.bfloat16)
    keys[64:64 + LAT, :] = own[:LAT, :]
    keys[64 + LAT:, :] = jnp.zeros((64, kb), jnp.bfloat16)
    copies[0].wait()
    copies[1].wait()
    causal = places[1:2, :].astype(jnp.float32) <= column(places[0:1, :rows], 0, rows)
    for j in range(chunks):
        if j % 2 == 0:
            copies[2 + j // 2].wait()
        lhs, first = chunk_rows(here, j, half)
        s = dot(lhs, keys[first:first + 640, :])
        for i in range(half):
            ex = jnp.exp2(s[i * rows:(i + 1) * rows] * (SCORE_SCALE * LOG2E))
            at = (j * half + i) * rows
            out[at:at + rows, :] = jnp.where(causal, ex, 0.0)


def block_kernel(half, q, block, out, keys):
    rows, kb = q.shape[0], block.shape[1]
    keys[:64, :] = jnp.zeros((64, kb), jnp.bfloat16)
    keys[64:64 + LAT, :] = block[:LAT, :]
    keys[64 + LAT:, :] = jnp.zeros((64, kb), jnp.bfloat16)
    size = half * rows
    for j in range(q.shape[1] // (half * LAT)):
        lhs, first = chunk_rows(q, j, half)
        out[j * size:(j + 1) * size, :] = jnp.exp2(dot(lhs, keys[first:first + 640, :]) * (SCORE_SCALE * LOG2E))


def main_kernel(half, place, q, own, a, b, c, own_exp, b_exp, outside, qpos, kpos, *rest):
    outs, rest = rest[:GROUPS], rest[GROUPS:]
    e, inv, (keys, out_exp, mass) = rest[:BUFFERS], rest[BUFFERS:2 * BUFFERS], rest[2 * BUFFERS:]
    z, position = place[0], place[1]
    rows, kb = q.shape[0], own.shape[1]
    chunks = q.shape[1] // (half * LAT)
    window = STEPS * kb
    own_slot, a_slot, b_slot, c_slot = slots_of(position)
    slots = (a_slot, c_slot, b_slot, own_slot)
    present = [position >= STEPS - 1 - slot for slot in slots]
    later = 2
    done = {later: b_exp, later + 1: own_exp}
    lane = lax.broadcasted_iota(jnp.int32, (32, 128), 1)

    keys[:64, :] = jnp.zeros((64, window), jnp.bfloat16)
    keys[64 + LAT:, :] = jnp.zeros((64, window), jnp.bfloat16)
    for i, block in enumerate((a, c)):
        keys[64:64 + LAT, i * kb:(i + 1) * kb] = block[:LAT, :]
    out_exp[...] = jnp.exp(turned_tall(outside[...], NEGATIVE))
    mass[...] = jnp.zeros_like(mass)
    worst = [jnp.zeros((32, 1), jnp.float32)]

    def exp_unit(j, i, r):
        buffer, at = j % BUFFERS, i * rows + r
        done_rows = slice(j * half * rows + at, j * half * rows + at + 32)
        head = (j - j % 2) * half + 2 * i + j % 2
        total = jnp.where(lane == head, out_exp[r:r + 32, :], 0.0)
        for block in range(STEPS):
            if block in done:
                piece = done[block][done_rows, :]
            else:
                piece = e[buffer][at:at + 32, block * kb:(block + 1) * kb]
            sums = piece[:, :128]
            for k in range(128, kb, 128):
                sums = sums + piece[:, k:k + 128]
            total = total + (sums if block == STEPS - 1 else jnp.where(present[block], sums, 0.0))
        total = jnp.sum(total, axis=1, keepdims=True)
        inv[buffer][at:at + 32, :] = jnp.broadcast_to(1.0 / total, (32, 128))
        worst[0] = jnp.maximum(worst[0], total)

    def mass_unit(j, r, w):
        buffer = j % BUFFERS
        total = mass[r:r + 32, w:w + 2 * kb]
        for i in range(half):
            at = i * rows + r
            if w // kb in done:
                first = j * half * rows + at
                piece = jnp.concatenate([done[w // kb + k][first:first + 32, :] for k in range(2)], 1)
            else:
                piece = e[buffer][at:at + 32, :]
            scale = inv[buffer][at:at + 32, :]
            total = total + piece * jnp.concatenate([scale] * (2 * kb // 128), 1)
        mass[r:r + 32, w:w + 2 * kb] = total

    exps = [(i, r) for i in range(half) for r in range(0, rows, 32)]
    sums = [(r, w) for r in range(0, rows, 32) for w in range(0, window, 2 * kb)]
    thirds = later
    for j in range(chunks + 2):
        if j < chunks:
            lhs, first = chunk_rows(q, j, half)
        for n in range(thirds):
            if j < chunks:
                lanes = slice(n * kb, (n + 1) * kb)
                s = dot(lhs, keys[first:first + 640, lanes])
                e[j % BUFFERS][:, lanes] = jnp.exp2(s * (SCORE_SCALE * LOG2E))
            if 1 <= j <= chunks:
                for i, r in exps[n * len(exps) // thirds:(n + 1) * len(exps) // thirds]:
                    exp_unit(j - 1, i, r)
            if j >= 2:
                for r, w in sums[n * len(sums) // thirds:(n + 1) * len(sums) // thirds]:
                    mass_unit(j - 2, r, w)

    @pl.when(jnp.logical_not(jnp.max(worst[0]) < SAFE))
    def _():
        for i, block in enumerate((b, own)):
            keys[64:64 + LAT, (later + i) * kb:(later + i + 1) * kb] = block[:LAT, :]
        causal = kpos[...].astype(jnp.float32) <= column(qpos[...], 0, rows)
        seen = [jnp.where(p, jnp.ones((rows, kb), jnp.float32), 0.0) for p in present[:STEPS - 1]]
        visible = jnp.concatenate(seen + [jnp.where(causal, 1.0, 0.0)], 1) > 0
        line = lax.broadcasted_iota(jnp.int32, outside.shape, 0)
        mass[...] = jnp.zeros_like(mass)
        for parity in range(2):

            def exact(i, carry, parity=parity):
                first = 64 - 64 * parity
                at = pl.multiple_of(1152 * i + 512 * parity, 128)
                scores = dot(q[:, pl.ds(at, 640)], keys[first:first + 640, :]) * SCORE_SCALE
                masked = jnp.where(visible, scores, NEGATIVE)
                mine = jnp.sum(jnp.where(line == 2 * i + parity, outside[...], 0.0), axis=0, keepdims=True)
                mine = column(mine, 0, rows)
                top = jnp.maximum(jnp.max(masked, axis=1, keepdims=True), mine)
                ex = jnp.exp(masked - top)
                total = jnp.sum(ex, axis=1, keepdims=True) + jnp.exp(mine - top)
                mass[...] += ex * (1.0 / total)
                return carry

            lax.fori_loop(0, outside.shape[0] // 2, exact, 0)

    ordered = [mass[:, i * kb:(i + 1) * kb] for i in range(STEPS)]
    ordered = [x if i == STEPS - 1 else jnp.where(present[i], x, 0.0) for i, x in enumerate(ordered)]
    for slot, x in zip(slots, ordered):
        mass[:, pl.ds(pl.multiple_of(slot * kb, kb), kb)] = x
    share = rows // GROUPS
    for d in range(GROUPS):
        at = pl.ds(pl.multiple_of((z ^ d) * share, share), share)
        if d == 0:
            outs[d][...] = mass[at, :]
        else:
            coded_rows(outs[d], mass[at, :])


def heads_of(piece, count):
    return jnp.concatenate([piece[:, IDIM * j:IDIM * (j + 1)] for j in range(count)], 0)


def index_kernel(count, place, own, a, b, c, *rest):
    pieces, (score, gate, turned, keys) = rest[:GROUPS], rest[GROUPS:]
    share = score.shape[0]
    tile = count * share
    gathered(place[1], (own, a, b, c), keys)
    total = jnp.zeros(score.shape, jnp.float32)
    for d in range(GROUPS):
        piece = pieces[d][...]
        scaled = weights_of(piece, IDIM * count, count) * (IDIM ** -0.5)
        rows = heads_of(piece, count)
        act = dot(rows, keys[...])
        gate[d * tile:(d + 1) * tile, :] = jnp.where(act > 0, 1.0, 0.0).astype(jnp.bfloat16)
        for j in range(count):
            total = total + jnp.maximum(act[j * share:(j + 1) * share], 0.0) * scaled[:, j:j + 1]
        tall = jnp.concatenate([jnp.broadcast_to(scaled[:, j:j + 1], (share, IDIM)) for j in range(count)], 0)
        high, low = split(rows.astype(jnp.float32) * tall)
        turned[:IDIM, d * tile:(d + 1) * tile] = high.T
        turned[IDIM:, d * tile:(d + 1) * tile] = low.T
    score[...] = total


def dscore_kernel(place, m0, m3, m2, m1, score, outside, qpos, kpos, spread, code):
    z, position = place[0], place[1]
    share, window = score.shape
    kb = kpos.shape[1]
    mass = (m0[...] + restored_rows(m1, window)) + (restored_rows(m2, window) + restored_rows(m3, window))
    target = mass / jnp.sum(mass, axis=1, keepdims=True)
    slot = lax.broadcasted_iota(jnp.int32, (share, window), 1) // kb
    causal = kpos[...].astype(jnp.float32) <= column(qpos[...], z * share, share)
    masked = jnp.where(position >= STEPS - 1 - slot, score[...], NEGATIVE)
    masked = jnp.concatenate([masked[:, :window - kb], jnp.where(causal, masked[:, window - kb:], NEGATIVE)], 1)
    out = column(outside[...], z * share, share)
    top = jnp.maximum(jnp.max(masked, axis=1, keepdims=True), out)
    expo = jnp.exp(masked - top)
    total = jnp.sum(expo, axis=1, keepdims=True) + jnp.exp(out - top)
    dscore = (expo / total - target) * float(window)
    spread[0], spread[1] = split(dscore)
    coded_rows(code, dscore)


def keys_kernel(count, gate, turned, spread, *outs):
    tile = count * spread.shape[1]
    total = None
    for d in range(GROUPS):
        rows = slice(d * tile, (d + 1) * tile)
        mask = gate[rows, :]
        both = dot(turned[:, rows], mask * jnp.concatenate([spread[0]] * count, 0))
        low = dot(turned[:IDIM, rows], mask * jnp.concatenate([spread[1]] * count, 0))
        part = both[:IDIM] + both[IDIM:] + low
        total = part if total is None else total + part
    kb = outs[STEPS - 1].shape[0]
    for i in range(STEPS):
        part = total[:, i * kb:(i + 1) * kb].T
        if i < STEPS - 1:
            coded_columns(outs[i], part)
        else:
            outs[i][...] = part


def query_kernel(heads, group, place, own, a, b, c, query, weight, c0, c1, c2, c3, *rest):
    first = heads[0]
    if first:
        (done, before), rest = rest[:2], rest[2:]
    grad, out, keys, turned, high, low, scale, tall = rest
    share, rows = c0.shape[0], query.shape[0]
    window = keys.shape[1]
    gathered(place[1], (own, a, b, c), keys)
    turned[...] = keys[...].T
    for d, code in enumerate((c0, c1, c2, c3)):
        at = pl.ds(pl.multiple_of((place[0] ^ d) * share, share), share)
        high[at, :], low[at, :] = split(code[:, :window].astype(jnp.float32))
        scale[at, :] = scale_of(code[:, window:]) * (IDIM ** -0.5)
    tall[...] = turned_tall(weight[...])
    lane = lax.broadcasted_iota(jnp.int32, (rows, 128), 1)
    total = before[...] if first else jnp.zeros((rows, 128), jnp.float32)
    if first:
        grad[:, :IDIM * first] = done[:, :IDIM * first]
    for g in range(*heads, group):
        tile = heads_of(query[:, IDIM * g:IDIM * (g + group)], group)
        mask = jnp.where(dot(tile, keys[...]) > 0, 1.0, 0.0).astype(jnp.bfloat16)
        part = dot(mask * jnp.concatenate([high[...]] * group, 0), turned[...])
        part = part + dot(mask * jnp.concatenate([low[...]] * group, 0), turned[...])
        for j in range(g, g + group):
            lanes = slice(IDIM * j, IDIM * (j + 1))
            mine = part[(j - g) * rows:(j - g + 1) * rows] * scale[...]
            grad[:, lanes] = (mine * tall[:, j:j + 1]).astype(jnp.bfloat16)
            product = jnp.sum(mine * query[:, lanes].astype(jnp.float32), axis=1, keepdims=True)
            total = jnp.where(lane == j, product, total)
    out[...] = total.T[:out.shape[0], :] if out.shape[0] < rows else total


def owned_kernel(p0, c1, c2, c3, code):
    kb = p0.shape[0]
    moved = [restored_columns(c, kb) for c in (c1, c2, c3)]
    coded_columns(code, (p0[...] + moved[0]) + (moved[1] + moved[2]))


def total_kernel(c0, c1, c2, c3, out):
    parts = [restored_columns(c, out.shape[0]) for c in (c0, c1, c2, c3)]
    out[...] = (parts[0] + parts[1]) + (parts[2] + parts[3])


SMEM = pl.BlockSpec(memory_space=pltpu.SMEM)
HBM = pl.BlockSpec(memory_space=pltpu.HBM)


def held(array):
    return pltpu.with_memory_space_constraint(array, pltpu.HBM)


def whole(array):
    rank = len(array.shape)
    return pl.BlockSpec(array.shape, lambda i: (0,) * rank)


def params(mib):
    return pltpu.CompilerParams(vmem_limit_bytes=mib << 20)


def cost(flops, size):
    return pl.CostEstimate(flops=1, bytes_accessed=1, transcendentals=0)


def along(x, axis, route):
    size = lax.axis_size(axis)
    return lax.ppermute(x, axis, [(i, j % size) for i, j in route])


def shards(
    main_query,
    latent,
    main_outside,
    index_query,
    index_weights,
    index_keys,
    index_outside,
    query_pos,
    key_pos,
):
    rows = main_query.shape[0]
    kb = latent.shape[0]
    heads = main_outside.shape[1]
    count = index_weights.shape[1]
    share = rows // GROUPS
    window = STEPS * kb
    n_seq = lax.axis_size("seq")
    z, position = lax.axis_index("head"), lax.axis_index("seq")
    place = jnp.stack([z, position]).astype(jnp.int32)
    bf16, f32, int16 = jnp.bfloat16, jnp.float32, jnp.int16

    def shape(dims, kind):
        return jax.ShapeDtypeStruct(dims, kind)

    def exchanged(x, d):
        return along(x, "head", [(i, i ^ d) for i in range(GROUPS)])

    weights = index_weights.T
    outsides = main_outside.T
    qpos = query_pos.reshape(1, rows)
    kpos = key_pos.reshape(1, kb)
    outside = index_outside.reshape(1, rows)
    piece_shape = (share, IDIM * count + 128)
    packed = latent.T
    to_b = [(i, i + (3 if i % 2 == 0 else 1)) for i in range(n_seq)]
    to_a = [(i, i + (1 if i % 2 == 0 else 3)) for i in range(n_seq)]
    to_c = [(i, i ^ 1) for i in range(n_seq)]
    route_b = along(packed, "seq", to_b)
    turned_shape = (IDIM, kb)
    both_shape = (LAT + IDIM, kb)
    both, turned_keys, *mine = pl.pallas_call(
        pack_kernel,
        grid=(1,),
        in_specs=[SMEM] + [HBM] * 4,
        out_specs=[pl.BlockSpec(both_shape, lambda i: (0, 0)), pl.BlockSpec(turned_shape, lambda i: (0, 0))]
        + [pl.BlockSpec(piece_shape, lambda i: (0, 0))] * GROUPS,
        out_shape=[shape(both_shape, bf16), shape(turned_shape, bf16)] + [shape(piece_shape, bf16)] * GROUPS,
        scratch_shapes=[
            pltpu.VMEM((rows, 128), bf16),
            pltpu.VMEM((count, rows), f32),
            pltpu.VMEM((kb, IDIM), bf16),
            pltpu.SemaphoreType.DMA((GROUPS + 3,)),
        ],
        compiler_params=params(16),
        cost_estimate=cost(0, 4 * rows * count * IDIM),
        name="pack_rows",
    )(place, *[held(x) for x in (packed, index_keys, index_query, weights)])
    route_a = along(both, "seq", to_a)
    pieces = [mine[0]] + [exchanged(mine[d], d) for d in range(1, GROUPS)]

    half = PER_STEP // 2
    own_exp = pl.pallas_call(
        functools.partial(own_kernel, half),
        grid=(1,),
        in_specs=[HBM, whole(packed), HBM, HBM],
        out_specs=pl.BlockSpec((heads * rows, kb), lambda i: (0, 0)),
        out_shape=shape((heads * rows, kb), f32),
        scratch_shapes=[
            pltpu.VMEM((704, kb), bf16),
            pltpu.VMEM(main_query.shape, bf16),
            pltpu.VMEM((8, kb), jnp.int32),
            pltpu.SemaphoreType.DMA((heads // PER_STEP + 2,)),
        ],
        compiler_params=params(24),
        cost_estimate=cost(2 * heads * rows * kb * LAT, heads * rows * (2 * LAT + 4 * kb)),
        name="own_block",
    )(held(main_query), packed, held(qpos), held(kpos))

    route_b, own_exp, pieces[1] = lax.optimization_barrier((route_b, own_exp, pieces[1]))
    b_exp = pl.pallas_call(
        functools.partial(block_kernel, half),
        grid=(1,),
        in_specs=[whole(main_query), whole(route_b)],
        out_specs=pl.BlockSpec((heads * rows, kb), lambda i: (0, 0)),
        out_shape=shape((heads * rows, kb), f32),
        scratch_shapes=[pltpu.VMEM((704, kb), bf16)],
        compiler_params=params(16),
        cost_estimate=cost(2 * heads * rows * kb * LAT, heads * rows * (2 * LAT + 4 * kb)),
        name="next_block",
    )(main_query, route_b)
    route_c = along(route_b, "seq", to_c)
    blocks = (packed, route_a, route_b, route_c)
    sent_keys, b_exp = lax.optimization_barrier((turned_keys, b_exp))
    keys_b = along(sent_keys, "seq", to_b)
    key_rows = (turned_keys, route_a, keys_b, along(keys_b, "seq", to_c))
    code_shape = (share, window + 128)
    mass = pl.pallas_call(
        functools.partial(main_kernel, half),
        grid=(1,),
        in_specs=[SMEM] + [whole(x) for x in (main_query, *blocks, own_exp, b_exp, outsides, qpos, kpos)],
        out_specs=[pl.BlockSpec((share, window), lambda i: (0, 0))]
        + [pl.BlockSpec(code_shape, lambda i: (0, 0))] * (GROUPS - 1),
        out_shape=[shape((share, window), f32)] + [shape(code_shape, int16)] * (GROUPS - 1),
        scratch_shapes=[pltpu.VMEM((half * rows, 2 * kb), f32)] * BUFFERS
        + [pltpu.VMEM((half * rows, 128), f32)] * BUFFERS
        + [
            pltpu.VMEM((704, window), bf16),
            pltpu.VMEM((rows, 128), f32),
            pltpu.VMEM((rows, window), f32),
        ],
        compiler_params=params(32),
        cost_estimate=cost(2 * heads * rows * window * LAT, heads * rows * 2 * LAT),
        name="main_mass",
    )(place, main_query, *blocks, own_exp, b_exp, outsides, qpos, kpos)
    masses = [mass[0]] + [exchanged(mass[d], d) for d in range(1, GROUPS)]

    tile = count * share
    score, gate, turned = pl.pallas_call(
        functools.partial(index_kernel, count),
        grid=(1,),
        in_specs=[SMEM] + [whole(x) for x in key_rows] + [whole(x) for x in pieces],
        out_specs=[
            pl.BlockSpec((share, window), lambda i: (0, 0)),
            pl.BlockSpec((GROUPS * tile, window), lambda i: (0, 0)),
            pl.BlockSpec((2 * IDIM, GROUPS * tile), lambda i: (0, 0)),
        ],
        out_shape=[
            shape((share, window), f32),
            shape((GROUPS * tile, window), bf16),
            shape((2 * IDIM, GROUPS * tile), bf16),
        ],
        scratch_shapes=[pltpu.VMEM((IDIM, window), bf16)],
        compiler_params=params(24),
        cost_estimate=cost(4 * GROUPS * tile * window * IDIM, GROUPS * tile * window * 2),
        name="index_scores",
    )(place, *key_rows, *pieces)

    spread, code = pl.pallas_call(
        dscore_kernel,
        grid=(1,),
        in_specs=[SMEM] + [whole(x) for x in (masses[0], *masses[:0:-1], score, outside, qpos, kpos)],
        out_specs=[
            pl.BlockSpec((2, share, window), lambda i: (0, 0, 0)),
            pl.BlockSpec(code_shape, lambda i: (0, 0)),
        ],
        out_shape=[shape((2, share, window), bf16), shape(code_shape, int16)],
        compiler_params=params(16),
        cost_estimate=cost(0, 12 * share * window),
        name="dscores",
    )(place, masses[0], *masses[:0:-1], score, outside, qpos, kpos)

    sum_shape = (kb + 16, IDIM)
    parts = pl.pallas_call(
        functools.partial(keys_kernel, count),
        grid=(1,),
        in_specs=[whole(gate), whole(turned), whole(spread)],
        out_specs=[pl.BlockSpec(sum_shape, lambda i: (0, 0))] * (STEPS - 1)
        + [pl.BlockSpec((kb, IDIM), lambda i: (0, 0))],
        out_shape=[shape(sum_shape, int16)] * (STEPS - 1) + [shape((kb, IDIM), f32)],
        compiler_params=params(24),
        cost_estimate=cost(8 * GROUPS * tile * window * IDIM, GROUPS * tile * window * 2),
        name="key_grads",
    )(gate, turned, spread)
    own_part, code = lax.optimization_barrier((parts[STEPS - 1], code))
    codes = [code] + [exchanged(code, d) for d in range(1, GROUPS)]
    sent = [parts[STEPS - 1 - distance] for distance in range(1, STEPS)]
    moved = [along(x, "seq", [(i, i - d - 1) for i in range(n_seq)]) for d, x in enumerate(sent)]

    group = count // 4

    def query_grads(first, last, before):
        sums_shape = (count, rows) if last == count else (rows, 128)
        return pl.pallas_call(
            functools.partial(query_kernel, (first, last), group),
            grid=(1,),
            in_specs=[SMEM] + [whole(x) for x in key_rows]
            + [whole(x) for x in (index_query, weights, *codes)]
            + [whole(x) for x in before],
            out_specs=[
                pl.BlockSpec((rows, IDIM * count), lambda i: (0, 0)),
                pl.BlockSpec(sums_shape, lambda i: (0, 0)),
            ],
            out_shape=[shape((rows, IDIM * count), bf16), shape(sums_shape, f32)],
            scratch_shapes=[
                pltpu.VMEM((IDIM, window), bf16),
                pltpu.VMEM((window, IDIM), bf16),
                pltpu.VMEM((rows, window), bf16),
                pltpu.VMEM((rows, window), bf16),
                pltpu.VMEM((rows, 128), f32),
                pltpu.VMEM((rows, 128), f32),
            ],
            compiler_params=params(24),
            cost_estimate=cost(8 * rows * (last - first) * window * IDIM, 8 * rows * count * IDIM),
            name="query_grads",
        )(place, *key_rows, index_query, weights, *codes, *before)

    grad_query, grad_weight = query_grads(0, count, ())

    owned = pl.pallas_call(
        owned_kernel,
        grid=(1,),
        in_specs=[whole(x) for x in (own_part, *moved)],
        out_specs=pl.BlockSpec(sum_shape, lambda i: (0, 0)),
        out_shape=shape(sum_shape, int16),
        compiler_params=params(16),
        cost_estimate=cost(0, 20 * kb * IDIM),
        name="owned_keys",
    )(own_part, *moved)
    owners = [owned] + [exchanged(owned, d) for d in range(1, GROUPS)]
    grad_keys = pl.pallas_call(
        total_kernel,
        grid=(1,),
        in_specs=[whole(x) for x in owners],
        out_specs=pl.BlockSpec((kb, IDIM), lambda i: (0, 0)),
        out_shape=shape((kb, IDIM), f32),
        compiler_params=params(16),
        cost_estimate=cost(0, 12 * kb * IDIM),
        name="total_keys",
    )(*owners)
    return (grad_query, grad_weight.T, grad_keys)


def any_shards(main_query, latent, main_outside, index_query, index_weights, index_keys, *rest):
    args = (main_query, latent, main_outside, index_query, index_weights, index_keys, *rest)
    fits = (
        lax.axis_size("head") == GROUPS
        and lax.axis_size("seq") % 2 == 0
        and main_query.shape[0] == 128
        and main_outside.shape[1] % PER_STEP == 0
        and main_outside.shape[1] <= 128
        and latent.shape[0] % 256 == 0
        and latent.shape[1] == LAT
        and 3 * index_weights.shape[1] <= 128
        and index_weights.shape[1] % 16 == 0
    )
    return shards(*args) if fits else plain_shards(*args)


def solution(mesh):
    in_specs = (
        P("seq", "head"),
        P("seq", None),
        P("seq", "head"),
        P("seq", "head"),
        P("seq", "head"),
        P("seq", None),
        P("seq"),
        P("seq"),
        P("seq"),
    )
    out_specs = (P("seq", "head"), P("seq", "head"), P("seq", None))
    return jax.shard_map(any_shards, mesh=mesh, in_specs=in_specs, out_specs=out_specs, check_vma=False)
```
